32 devices in a mesh: groups: 2 (over x), sect: 8 (over z, y), tp: 2 (over core).
Axes of the slice: x: 2, y: 2, z: 4, core: 2. Of those that a mesh axis runs over, the one named last changes fastest.
Arguments:
- hidden_in: bfloat16 [512, 4096], P(('groups', 'sect')), parts along dimension 0, may hold values from -6 to 6
- expert_ids: int32 [512, 8], P(('groups', 'sect')), parts along dimension 0, may hold values from 0 to 31, as said below
- route_scores: float32 [512, 8], P(('groups', 'sect')), parts along dimension 0, may hold values from 0.1 to 1
- expert_slot: int32 [32], replicated, may hold values from 0 to 31, each once
- gate_matrix: bfloat16 [32, 4096, 1024], P('sect', None, 'tp'), may hold values from -0.09375 to 0.09375
- up_matrix: bfloat16 [32, 4096, 1024], P('sect', None, 'tp'), may hold values from -0.09375 to 0.09375
- down_matrix: bfloat16 [32, 1024, 4096], P('sect', 'tp'), may hold values from -0.1875 to 0.1875
Outputs:
- mixed: bfloat16 [512, 4096], P(('groups', 'sect'), 'tp'), parts along dimension 0
The draws below stay inside these ranges and needn't reach their ends.
There are 2 independent parts, one for each index of `groups`. The reference program is written for one: setup_inputs(seed, part) draws one part's arguments, and reference() takes and returns one part's arrays. A program takes and returns all parts, laid end to end along the dimension named above; an argument that names none is the same for every part. Nothing has to cross between parts.
Inputs may be any that keep to these rules, and one draw needn't show every extreme that they name: `expert_ids`: each row names 8 different experts; the 32 rows of one device name any expert at most 16 times, and on every device one or more experts exactly 16 times.
All inputs are finite; a program needn't handle non-finite values.
Results may differ from the reference program's by a relative error of at most 0.0031.
Values may be sent and summed in bfloat16 or wider, within the bound.
No kernel may reach another device: no remote copies, remote signals or barrier semaphores. Data moves between devices by JAX's collectives and lax.ppermute only.
A program may use at most 128 MiB of HBM per device.

```python
import math
import jax
import jax.numpy as jnp
from jax import lax

D = 4096
FF = 1024
TOP = 8
EXPERTS = 32
B_DEV = 32
CAP = 16
TOKENS = 256
N_SECT = 8


def draw_expert_ids(key, part):
    key = jax.random.fold_in(key, 11)
    key_common, key_rest = jax.random.split(key)
    common = jax.random.randint(key_common, (), 0, EXPERTS).astype(jnp.int32)
    block_count = TOKENS // B_DEV
    entry_total = B_DEV * TOP

    def one_block(block_key):
        key_one, key_two, key_three, key_four, key_five = jax.random.split(block_key, 5)
        rank = jnp.arange(EXPERTS, dtype=jnp.int32)
        hot_count = jax.random.randint(key_one, (), 1, EXPERTS // 4 + 1).astype(jnp.int32)
        is_hot = rank < hot_count
        others = EXPERTS - hot_count
        rest = entry_total - hot_count * CAP
        base = rest // others
        extra = rest - base * others
        other_rank = rank - hot_count
        even = base + (other_rank < extra).astype(jnp.int32)
        even = jnp.where(is_hot, jnp.zeros_like(even), even)
        partner_rank = jnp.bitwise_xor(jnp.maximum(other_rank, 0), 1)
        partner_idx = jnp.clip(partner_rank + hot_count, 0, EXPERTS - 1)
        paired = jnp.logical_not(is_hot) & (partner_rank < others)
        pair_sum = even + even[partner_idx]
        lower = jnp.where(paired, jnp.maximum(pair_sum - (CAP - 1), 0), 0)
        upper = jnp.where(paired, jnp.minimum(pair_sum, CAP - 1), 0)
        moved = jax.random.randint(key_two, (EXPERTS,), lower, upper + 1).astype(jnp.int32)
        is_low = paired & (jnp.maximum(other_rank, 0) % 2 == 0)
        counts = jnp.where(is_hot, CAP, jnp.where(is_low, moved, jnp.where(paired, pair_sum - moved[partner_idx], even))).astype(jnp.int32)
        ends = jnp.cumsum(counts)
        entry_pos = jnp.arange(entry_total, dtype=jnp.int32)
        entry_rank = jnp.sum((entry_pos[:, None] >= ends[None, :]).astype(jnp.int32), axis=1)
        labels = jax.random.permutation(key_three, EXPERTS).astype(jnp.int32)
        labels = jnp.where(rank == 0, common, jnp.where(labels == common, labels[0], labels))
        entry_expert = labels[entry_rank]
        grid = entry_expert.reshape(TOP, B_DEV).T
        grid = grid[jax.random.permutation(key_four, B_DEV)]
        shifts = jax.random.randint(key_five, (B_DEV,), 0, TOP)
        rolled = (jnp.arange(TOP, dtype=jnp.int32)[None, :] + shifts[:, None]) % TOP
        return jnp.take_along_axis(grid, rolled, axis=1)
    blocks = jax.vmap(one_block)(jax.random.split(key_rest, block_count))
    return blocks.reshape(TOKENS, TOP).astype(jnp.int32)


def level_of(key, shape, shards, least, high):
    def one(dim, blocks):
        heights = jax.random.uniform(jax.random.fold_in(jax.random.fold_in(key, 6), dim), (blocks,), jnp.float32, least / len(shards), high / len(shards))
        return jnp.repeat(jnp.exp(heights), shape[dim] // blocks).reshape((-1,) + (1,) * (len(shape) - dim - 1))

    loudness = one(*shards[0])
    for cut in shards[1:]:
        loudness = loudness * one(*cut)
    return loudness


def scatter_about(stream_key, extent, spread, reach, cuts=(), kind=jnp.bfloat16):
    array = spread * jax.random.normal(stream_key, extent, jnp.float32)
    if cuts:
        array = array * level_of(stream_key, extent, cuts, -0.22, 0.18)
    return jnp.clip(array, -reach, reach).astype(kind)


def setup_inputs(seed: int = 0, part: int = 0) -> dict:
    arg_keys = jax.random.split(jax.random.key(seed), 8)
    part_splits = jax.random.split(jax.random.fold_in(arg_keys[7], part), 8)
    return {
        "hidden_in": scatter_about(part_splits[0], (TOKENS, D), 1.0, 6.0, ((0, 8),)),
        "expert_ids": draw_expert_ids(jax.random.fold_in(jax.random.fold_in(arg_keys[7], part), 71), part),
        "route_scores": jnp.clip(jnp.exp(math.log(1.0) - 2.3025851 * jax.random.uniform(part_splits[2], (TOKENS, TOP), jnp.float32) ** level_of(part_splits[2], (TOKENS, TOP), ((0, 8),), -0.2, 0.2)), 0.1, 1.0),
        "expert_slot": jax.random.permutation(arg_keys[3], EXPERTS).astype(jnp.int32),
        "gate_matrix": scatter_about(arg_keys[4], (EXPERTS, D, FF), D ** -0.5, 0.09375, ((0, 8), (2, 2))),
        "up_matrix": scatter_about(arg_keys[5], (EXPERTS, D, FF), D ** -0.5, 0.09375, ((0, 8), (2, 2))),
        "down_matrix": scatter_about(arg_keys[6], (EXPERTS, FF, D), FF ** -0.5, 0.1875, ((0, 8), (1, 2))),
    }


def reference(hidden_in, expert_ids, route_scores, expert_slot, gate_matrix, up_matrix, down_matrix):
    resid = hidden_in.astype(jnp.float32)
    normed = (resid * lax.rsqrt(lax.optimization_barrier(jnp.mean(resid * resid, axis=-1, keepdims=True)) + 1e-06)).astype(jnp.bfloat16)
    mixing = route_scores / lax.optimization_barrier(jnp.sum(route_scores, axis=-1, keepdims=True))
    row_limit = N_SECT * CAP

    def per_expert(running, expert):
        matched = expert_ids == expert
        weight_col = lax.optimization_barrier(jnp.sum(jnp.where(matched, mixing, jnp.zeros_like(mixing)), axis=-1))
        chosen = jnp.any(matched, axis=-1).astype(jnp.int32)
        taken = jnp.argsort(1 - chosen, stable=True)[:row_limit]
        arrived = normed[taken]
        slot = expert_slot[expert]
        gate_mat = lax.dynamic_index_in_dim(gate_matrix, slot, 0, keepdims=False)
        up_mat = lax.dynamic_index_in_dim(up_matrix, slot, 0, keepdims=False)
        down_mat = lax.dynamic_index_in_dim(down_matrix, slot, 0, keepdims=False)
        gate_act = jnp.dot(arrived, gate_mat, preferred_element_type=jnp.float32)
        up_act = jnp.dot(arrived, up_mat, preferred_element_type=jnp.float32)
        hidden = (jax.nn.silu(gate_act) * up_act).astype(jnp.bfloat16)
        expert_out = jnp.dot(hidden, down_mat, preferred_element_type=jnp.float32).astype(jnp.bfloat16)
        contrib = weight_col[taken][:, None] * expert_out.astype(jnp.float32)
        return (running.at[taken].add(contrib), None)
    total, unused = lax.scan(per_expert, jnp.zeros(resid.shape, jnp.float32), jnp.arange(EXPERTS, dtype=jnp.int32))
    return (resid + total).astype(jnp.bfloat16)
```

```python
import functools

import jax
import jax.numpy as jnp
from jax import lax
from jax.experimental import pallas as pl
from jax.experimental.pallas import tpu as pltpu
from jax.sharding import PartitionSpec as P

LANES = 128


def prepare_kernel(half, experts, slot_ref, hidden_ref, own_ref, ids_ref, scores_ref, out_ref):
    resid = hidden_ref[...].astype(jnp.float32)
    scale = lax.rsqrt(jnp.mean(resid * resid, axis=-1, keepdims=True) + 1e-06)
    out_ref[:, :half] = (own_ref[...].astype(jnp.float32) * scale).astype(jnp.bfloat16)
    scores = scores_ref[...]
    mixing = scores / jnp.sum(scores, axis=-1, keepdims=True)
    ids = ids_ref[...]
    width = out_ref.shape[1] - half
    lane = lax.broadcasted_iota(jnp.int32, (1, width), 1)
    slot_of_lane = lax.rem(lane, experts)
    expert_of_lane = jnp.zeros((1, width), jnp.int32)
    for e in range(experts):
        expert_of_lane = jnp.where(slot_of_lane == slot_ref[e], e, expert_of_lane)
    weight = jnp.zeros((ids.shape[0], width), jnp.float32)
    for k in range(ids.shape[1]):
        weight = weight + jnp.where(ids[:, k : k + 1] == expert_of_lane, mixing[:, k : k + 1], 0.0)
    high = weight.astype(jnp.bfloat16)
    rest = weight - high.astype(jnp.float32)
    middle = rest.astype(jnp.bfloat16)
    low = (rest - middle.astype(jnp.float32)).astype(jnp.bfloat16)
    coded = jnp.where(
        lane < experts,
        high.astype(jnp.float32),
        jnp.where(
            lane < 2 * experts,
            middle.astype(jnp.float32),
            jnp.where(lane < 3 * experts, low.astype(jnp.float32), 0.0),
        ),
    )
    out_ref[:, half:] = coded.astype(jnp.bfloat16)


def prepare(hidden_in, own_half, expert_ids, route_scores, expert_slot):
    rows = hidden_in.shape[0]
    half = own_half.shape[1]
    experts = expert_slot.shape[0]
    width = -(-3 * experts // LANES) * LANES
    vmem = pl.BlockSpec(memory_space=pltpu.VMEM)
    return pl.pallas_call(
        functools.partial(prepare_kernel, half, experts),
        out_shape=jax.ShapeDtypeStruct((rows, half + width), jnp.bfloat16),
        in_specs=[pl.BlockSpec(memory_space=pltpu.SMEM), vmem, vmem, vmem, vmem],
        out_specs=vmem,
        compiler_params=pltpu.CompilerParams(vmem_limit_bytes=8 << 20),
        name="prepare",
    )(expert_slot, hidden_in, own_half, expert_ids, route_scores)


def experts_kernel(
    half, experts, place_ref, own_ref, other_ref, gate_ref, up_ref, down_ref, keep_ref, send_ref, acc
):
    e, f = pl.program_id(0), pl.program_id(1)
    last = (e == pl.num_programs(0) - 1) & (f == pl.num_programs(1) - 1)
    first_slot = place_ref[0] * pl.num_programs(0)
    core = place_ref[1]
    own_at = pl.ds(pl.multiple_of(core * half, half), half)
    other_at = pl.ds(pl.multiple_of((1 - core) * half, half), half)
    own, other = own_ref[:, :half], other_ref[...]

    def project(ref):
        return jnp.dot(
            own, ref[0, own_at, :], preferred_element_type=jnp.float32
        ) + jnp.dot(other, ref[0, other_at, :], preferred_element_type=jnp.float32)

    coded = own_ref[:, half:].astype(jnp.float32)
    lane = lax.broadcasted_iota(jnp.int32, coded.shape, 1)
    weight = jnp.sum(
        jnp.where(lax.rem(lane, experts) == first_slot + e, coded, 0.0), axis=1, keepdims=True
    )
    gate_act = project(gate_ref)
    up_act = project(up_ref)
    hidden = gate_act / (1.0 + jnp.exp(-gate_act)) * up_act
    hidden = jnp.where(weight > 0.0, hidden * weight, 0.0).astype(jnp.bfloat16)
    product = jnp.dot(hidden, down_ref[0], preferred_element_type=jnp.float32)

    @pl.when((e == 0) & (f == 0))
    def _():
        acc[...] = product

    @pl.when((e > 0) | (f > 0))
    def _():
        acc[...] += product

    @pl.when(last)
    def _():
        keep_ref[...] = acc[:, own_at]
        send_ref[...] = acc[:, other_at].astype(jnp.bfloat16)


def run_experts(place, own, other, gate_matrix, up_matrix, down_matrix, experts):
    rows, half = other.shape
    local, features, hidden_units = gate_matrix.shape
    cut = 2
    block = hidden_units // cut
    whole = lambda e, f, place: (0, 0)
    return pl.pallas_call(
        functools.partial(experts_kernel, half, experts),
        out_shape=(
            jax.ShapeDtypeStruct((rows, half), jnp.float32),
            jax.ShapeDtypeStruct((rows, half), jnp.bfloat16),
        ),
        grid_spec=pltpu.PrefetchScalarGridSpec(
            num_scalar_prefetch=1,
            grid=(local, cut),
            in_specs=[
                pl.BlockSpec(own.shape, whole),
                pl.BlockSpec(other.shape, whole),
                pl.BlockSpec((1, features, block), lambda e, f, place: (e, 0, f)),
                pl.BlockSpec((1, features, block), lambda e, f, place: (e, 0, f)),
                pl.BlockSpec((1, block, features), lambda e, f, place: (e, f, 0)),
            ],
            out_specs=[pl.BlockSpec((rows, half), whole), pl.BlockSpec((rows, half), whole)],
            scratch_shapes=[pltpu.VMEM((rows, features), jnp.float32)],
        ),
        compiler_params=pltpu.CompilerParams(vmem_limit_bytes=48 << 20),
        name="experts",
    )(place, own, other, gate_matrix, up_matrix, down_matrix)


def on_device(
    hidden_in, expert_ids, route_scores, expert_slot, gate_matrix, up_matrix, down_matrix
):
    token_count, feature_count = hidden_in.shape
    experts = expert_slot.shape[0]
    devices = lax.axis_size("sect")
    half = feature_count // 2
    core = lax.axis_index("tp")
    sect = lax.axis_index("sect")
    inner = 2
    outer = devices // inner

    def along(shift):
        return [
            (o * inner + i, (o + shift) % outer * inner + i)
            for o in range(outer)
            for i in range(inner)
        ]

    across = [(d, d ^ 1) for d in range(devices)]
    cores = [(0, 1), (1, 0)]

    own_half = lax.dynamic_slice_in_dim(hidden_in, core * half, half, 1)
    packed = prepare(hidden_in, own_half, expert_ids, route_scores, expert_slot)
    same = [packed] + [lax.ppermute(packed, "sect", along(k)) for k in range(1, outer)]
    opposite = [lax.ppermute(block, "sect", across) for block in same]
    blocks = same + opposite
    halves = [lax.ppermute(block[:, :half], "tp", cores) for block in blocks]
    own = jnp.concatenate(blocks, 0)
    other = jnp.concatenate(halves, 0)

    place = jnp.stack([sect, core]).astype(jnp.int32)
    total = own.shape[0]
    step = min(total, 256)
    keeps, sends = [], []
    for at in range(0, total, step):
        keep, send = run_experts(
            place, own[at : at + step], other[at : at + step], gate_matrix, up_matrix, down_matrix, experts
        )
        keeps.append(keep)
        sends.append(send)
    keep, send = jnp.concatenate(keeps, 0), jnp.concatenate(sends, 0)
    partial = keep + lax.ppermute(send, "tp", cores).astype(jnp.float32)
    partial = partial.reshape(inner, outer, token_count, half)
    result = own_half.astype(jnp.float32)
    for k in list(range(1, outer)) + [0]:
        crossed = lax.ppermute(partial[1, k].astype(jnp.bfloat16), "sect", across)
        block = partial[0, k] + crossed.astype(jnp.float32)
        if k:
            block = lax.ppermute(block.astype(jnp.bfloat16), "sect", along(-k)).astype(jnp.float32)
        result = result + block
    return result.astype(jnp.bfloat16)


def solution(mesh):
    placed = (
        P(("groups", "sect"), None),
        P(("groups", "sect"), None),
        P(("groups", "sect"), None),
        P(),
        P("sect", None, "tp"),
        P("sect", None, "tp"),
        P("sect", "tp", None),
    )
    return jax.shard_map(
        on_device,
        mesh=mesh,
        in_specs=placed,
        out_specs=P(("groups", "sect"), "tp"),
        check_vma=False,
    )
```

```python
import functools

import jax
import jax.numpy as jnp
from jax import lax
from jax.experimental import pallas as pl
from jax.experimental.pallas import tpu as pltpu
from jax.sharding import PartitionSpec as P

LANES = 128


def prepare_kernel(half, experts, place_ref, slot_ref, hidden_ref, ids_ref, scores_ref, out_ref):
    resid = hidden_ref[...].astype(jnp.float32)
    scale = lax.rsqrt(jnp.mean(resid * resid, axis=-1, keepdims=True) + 1e-06)
    own = hidden_ref[:, pl.ds(pl.multiple_of(place_ref[1] * half, half), half)]
    out_ref[:, :half] = (own.astype(jnp.float32) * scale).astype(jnp.bfloat16)
    scores = scores_ref[...]
    mixing = scores / jnp.sum(scores, axis=0, keepdims=True)
    ids = ids_ref[...]
    width = out_ref.shape[1] - half
    row = lax.broadcasted_iota(jnp.int32, (width, 1), 0)
    slot_of_row = lax.rem(row, experts)
    expert_of_row = jnp.zeros((width, 1), jnp.int32)
    for e in range(experts):
        expert_of_row = jnp.where(slot_of_row == slot_ref[e], e, expert_of_row)
    weight = jnp.zeros((width, ids.shape[1]), jnp.float32)
    for k in range(ids.shape[0]):
        weight = weight + jnp.where(ids[k : k + 1, :] == expert_of_row, mixing[k : k + 1, :], 0.0)
    high = weight.astype(jnp.bfloat16).astype(jnp.float32)
    middle = (weight - high).astype(jnp.bfloat16).astype(jnp.float32)
    low = weight - high - middle
    coded = jnp.where(
        row < experts,
        high,
        jnp.where(row < 2 * experts, middle, jnp.where(row < 3 * experts, low, 0.0)),
    )
    out_ref[:, half:] = coded.T.astype(jnp.bfloat16)


def prepare(place, hidden_in, expert_ids, route_scores, expert_slot):
    rows, features = hidden_in.shape
    half = features // 2
    experts = expert_slot.shape[0]
    width = -(-3 * experts // LANES) * LANES
    vmem = pl.BlockSpec(memory_space=pltpu.VMEM)
    smem = pl.BlockSpec(memory_space=pltpu.SMEM)
    return pl.pallas_call(
        functools.partial(prepare_kernel, half, experts),
        out_shape=jax.ShapeDtypeStruct((rows, half + width), jnp.bfloat16),
        in_specs=[smem, smem, vmem, vmem, vmem],
        out_specs=vmem,
        compiler_params=pltpu.CompilerParams(vmem_limit_bytes=8 << 20),
        name="prepare",
    )(place, expert_slot, hidden_in, expert_ids.T, route_scores.T)


def load_kernel(matrix_ref, *refs):
    out_refs, sem = refs[:-1], refs[-1]
    copies = [
        pltpu.make_async_copy(matrix_ref.at[i], out_ref, sem.at[i])
        for i, out_ref in enumerate(out_refs)
    ]
    for copy in copies:
        copy.start()
    for copy in copies:
        copy.wait()


def load(matrix):
    local = matrix.shape[0]
    return pl.pallas_call(
        load_kernel,
        out_shape=[pltpu.VMEM(matrix.shape[1:], matrix.dtype)] * local,
        in_specs=[pl.BlockSpec(memory_space=pltpu.HBM)],
        out_specs=[pl.BlockSpec(memory_space=pltpu.VMEM)] * local,
        scratch_shapes=[pltpu.SemaphoreType.DMA((local,))],
        compiler_params=pltpu.CompilerParams(vmem_limit_bytes=1 << 20),
        cost_estimate=pl.CostEstimate(flops=0, bytes_accessed=matrix.size // 8, transcendentals=0),
        name="load",
    )(pltpu.with_memory_space_constraint(matrix, pltpu.HBM))


def after(value, *others):
    return lax.optimization_barrier((value, *others))[0]


def hidden_kernel(half, experts, blocks, place_ref, *refs):
    own_refs, other_refs = refs[:blocks], refs[blocks : 2 * blocks]
    out_ref, own, other, coded = refs[-4:]
    weights = refs[2 * blocks : -4]
    local = len(weights) // 2
    gate_refs, up_refs = weights[:local], weights[local:]
    units = gate_refs[0].shape[1]
    first_slot = place_ref[0] * local
    own_at = pl.ds(pl.multiple_of(place_ref[1] * half, half), half)
    other_at = pl.ds(pl.multiple_of((1 - place_ref[1]) * half, half), half)
    tokens = own_refs[0].shape[0]
    for i in range(blocks):
        rows = slice(i * tokens, (i + 1) * tokens)
        own[rows, :] = own_refs[i][:, :half]
        other[rows, :] = other_refs[i][:, :half]
        coded[rows, :] = own_refs[i][:, half:].astype(jnp.float32)
    slot = lax.rem(lax.broadcasted_iota(jnp.int32, coded.shape, 1), experts)
    block = min(units, 256)
    for e in range(local):
        weight = jnp.sum(jnp.where(slot == first_slot + e, coded[...], 0.0), axis=1, keepdims=True)
        for at in range(0, units, block):
            cut = slice(at, at + block)

            def project(ref):
                return jnp.dot(
                    own[...], ref[own_at, cut], preferred_element_type=jnp.float32
                ) + jnp.dot(other[...], ref[other_at, cut], preferred_element_type=jnp.float32)

            gate_act = project(gate_refs[e])
            up_act = project(up_refs[e])
            hidden = gate_act / (1.0 + jnp.exp(-gate_act)) * up_act
            hidden = jnp.where(weight > 0.0, hidden * weight, 0.0)
            out_ref[:, e * units + at : e * units + at + block] = hidden.astype(jnp.bfloat16)


def run_hidden(place, own, other, gate, up, experts):
    blocks = len(own)
    rows, half = blocks * own[0].shape[0], gate[0].shape[0] // 2
    units = len(gate) * gate[0].shape[1]
    vmem = pl.BlockSpec(memory_space=pltpu.VMEM)
    return pl.pallas_call(
        functools.partial(hidden_kernel, half, experts, blocks),
        out_shape=jax.ShapeDtypeStruct((rows, units), jnp.bfloat16),
        in_specs=[pl.BlockSpec(memory_space=pltpu.SMEM)] + [vmem] * (2 * blocks + 2 * len(gate)),
        out_specs=vmem,
        scratch_shapes=[
            pltpu.VMEM((rows, half), jnp.bfloat16),
            pltpu.VMEM((rows, half), jnp.bfloat16),
            pltpu.VMEM((rows, own[0].shape[1] - half), jnp.float32),
        ],
        compiler_params=pltpu.CompilerParams(vmem_limit_bytes=6 << 20),
        cost_estimate=pl.CostEstimate(
            flops=4 * rows * units * 2 * half, bytes_accessed=rows * half * 4, transcendentals=rows * units
        ),
        name="hidden",
    )(place, *own, *other, *gate, *up)


def down_kernel(mine, place_ref, hidden_ref, *refs):
    out_ref = refs[-1]
    down_refs = refs[: -2 if mine else -1]
    local, (units, features) = len(down_refs), down_refs[0].shape
    half = features // 2
    core = place_ref[1] if mine else 1 - place_ref[1]
    block = 512
    for at in range(0, half, block):
        cut = pl.ds(pl.multiple_of(core * half + at, block), block)
        total = jnp.zeros((hidden_ref.shape[0], block), jnp.float32)
        for e in range(local):
            total = total + jnp.dot(
                hidden_ref[:, e * units : (e + 1) * units],
                down_refs[e][:, cut],
                preferred_element_type=jnp.float32,
            )
        if mine:
            total = total + refs[-2][:, at : at + block].astype(jnp.float32)
        out_ref[:, at : at + block] = total.astype(out_ref.dtype)


def run_down(place, hidden, down, received, kind):
    rows, half = hidden.shape[0], down[0].shape[1] // 2
    vmem = pl.BlockSpec(memory_space=pltpu.VMEM)
    extra = [] if received is None else [received]
    return pl.pallas_call(
        functools.partial(down_kernel, received is not None),
        out_shape=jax.ShapeDtypeStruct((rows, half), kind),
        in_specs=[pl.BlockSpec(memory_space=pltpu.SMEM), vmem] + [vmem] * len((*down, *extra)),
        out_specs=vmem,
        compiler_params=pltpu.CompilerParams(vmem_limit_bytes=6 << 20),
        cost_estimate=pl.CostEstimate(
            flops=2 * rows * half * hidden.shape[1], bytes_accessed=rows * half * 4, transcendentals=0
        ),
        name="down_mine" if extra else "down_other",
    )(place, hidden, *down, *extra)


def on_device(
    hidden_in, expert_ids, route_scores, expert_slot, gate_matrix, up_matrix, down_matrix
):
    token_count, feature_count = hidden_in.shape
    experts = expert_slot.shape[0]
    devices = lax.axis_size("sect")
    half = feature_count // 2
    core = lax.axis_index("tp")
    sect = lax.axis_index("sect")
    inner = 2
    outer = devices // inner

    def along(shift):
        return [
            (o * inner + i, (o + shift) % outer * inner + i)
            for o in range(outer)
            for i in range(inner)
        ]

    across = [(d, d ^ 1) for d in range(devices)]
    cores = [(0, 1), (1, 0)]
    place = jnp.stack([sect, core]).astype(jnp.int32)
    bf16, f32 = jnp.bfloat16, jnp.float32

    packed = prepare(place, hidden_in, expert_ids, route_scores, expert_slot)
    shifts = sorted(range(1, outer), key=lambda k: min(k, outer - k))
    early, late = shifts[: len(shifts) * 2 // 3], shifts[len(shifts) * 2 // 3 :]
    same, opposite = {0: packed}, {0: lax.ppermute(packed, "sect", across)}
    for k in shifts:
        same[k] = lax.ppermute(packed, "sect", along(k))
    gate_here = load(after(gate_matrix, packed))
    for k in early:
        opposite[k] = lax.ppermute(after(same[k], *gate_here), "sect", across)
    up_here = load(after(up_matrix, *gate_here, *[same[k] for k in early]))
    for k in late:
        opposite[k] = lax.ppermute(after(same[k], *up_here), "sect", across)
    down_here = load(after(down_matrix, *up_here, *[same[k] for k in late]))
    hidden = []
    for blocks in (same, opposite):
        blocks = [blocks[k] for k in range(outer)]
        halves = [lax.ppermute(block, "tp", cores) for block in blocks]
        if hidden:
            blocks[0] = after(blocks[0], hidden[0])
        hidden.append(run_hidden(place, blocks, halves, gate_here, up_here, experts))
    near, far = hidden
    far_send = lax.ppermute(run_down(place, far, down_here, None, bf16), "tp", cores)
    near_send = lax.ppermute(run_down(place, near, down_here, None, bf16), "tp", cores)
    far_sum = run_down(place, far, down_here, far_send, bf16)
    near_sum = run_down(place, near, down_here, near_send, f32)
    far_sum = far_sum.reshape(outer, token_count, half)
    near_sum = near_sum.reshape(outer, token_count, half)
    result = lax.dynamic_slice_in_dim(hidden_in, core * half, half, 1).astype(f32)
    order = sorted(range(1, outer), key=lambda k: -min(k, outer - k)) + [0]
    for k in order:
        block = near_sum[k] + lax.ppermute(far_sum[k], "sect", across).astype(f32)
        if k:
            block = lax.ppermute(block.astype(bf16), "sect", along(-k)).astype(f32)
        result = result + block
    return result.astype(bf16)


def solution(mesh):
    placed = (
        P(("groups", "sect"), None),
        P(("groups", "sect"), None),
        P(("groups", "sect"), None),
        P(),
        P("sect", None, "tp"),
        P("sect", None, "tp"),
        P("sect", "tp", None),
    )
    return jax.shard_map(
        on_device,
        mesh=mesh,
        in_specs=placed,
        out_specs=P(("groups", "sect"), "tp"),
        check_vma=False,
    )
```

```python
import functools

import jax
import jax.numpy as jnp
from jax import lax
from jax.experimental import pallas as pl
from jax.experimental.pallas import tpu as pltpu
from jax.sharding import PartitionSpec as P

LANES = 128
WIDTH = 512
LEAD_FLOPS = 40_000_000_000


def prepare_kernel(half, experts, place_ref, *refs):
    out_ref, slot_ref, hidden_ref, ids_ref, scores_ref, sem = refs[4:]
    copies = [
        pltpu.make_async_copy(refs[i], refs[5 + i], sem.at[i]) for i in range(4)
    ]
    for copy in copies:
        copy.start()
    for copy in copies:
        copy.wait()
    resid = hidden_ref[...].astype(jnp.float32)
    scale = lax.rsqrt(jnp.mean(resid * resid, axis=-1, keepdims=True) + 1e-06)
    own = hidden_ref[:, pl.ds(pl.multiple_of(place_ref[1] * half, half), half)]
    out_ref[:, :half] = (own.astype(jnp.float32) * scale).astype(jnp.bfloat16)
    scores = scores_ref[...]
    mixing = scores / jnp.sum(scores, axis=0, keepdims=True)
    ids = ids_ref[...]
    width = out_ref.shape[1] - half
    row = lax.broadcasted_iota(jnp.int32, (width, 1), 0)
    slot_of_row = lax.rem(row, experts)
    expert_of_row = jnp.zeros((width, 1), jnp.int32)
    for e in range(experts):
        expert_of_row = jnp.where(slot_of_row == slot_ref[e], e, expert_of_row)
    weight = jnp.zeros((width, ids.shape[1]), jnp.float32)
    for k in range(ids.shape[0]):
        weight = weight + jnp.where(ids[k : k + 1, :] == expert_of_row, mixing[k : k + 1, :], 0.0)
    high = weight.astype(jnp.bfloat16).astype(jnp.float32)
    middle = (weight - high).astype(jnp.bfloat16).astype(jnp.float32)
    low = weight - high - middle
    coded = jnp.where(
        row < experts,
        high,
        jnp.where(row < 2 * experts, middle, jnp.where(row < 3 * experts, low, 0.0)),
    )
    out_ref[:, half:] = coded.T.astype(jnp.bfloat16)


def prepare(place, hidden_in, expert_ids, route_scores, expert_slot):
    rows, features = hidden_in.shape
    half = features // 2
    experts = expert_slot.shape[0]
    width = -(-3 * experts // LANES) * LANES
    vmem = pl.BlockSpec(memory_space=pltpu.VMEM)
    smem, hbm = pl.BlockSpec(memory_space=pltpu.SMEM), pl.BlockSpec(memory_space=pltpu.HBM)
    far = [expert_slot, hidden_in, expert_ids.T, route_scores.T]
    far = [pltpu.with_memory_space_constraint(a, pltpu.HBM) for a in far]
    return pl.pallas_call(
        functools.partial(prepare_kernel, half, experts),
        out_shape=jax.ShapeDtypeStruct((rows, half + width), jnp.bfloat16),
        in_specs=[smem, hbm, hbm, hbm, hbm],
        out_specs=vmem,
        scratch_shapes=[
            pltpu.SMEM(expert_slot.shape, jnp.int32),
            pltpu.VMEM(hidden_in.shape, hidden_in.dtype),
            pltpu.VMEM(expert_ids.shape[::-1], jnp.int32),
            pltpu.VMEM(route_scores.shape[::-1], jnp.float32),
            pltpu.SemaphoreType.DMA((4,)),
        ],
        compiler_params=pltpu.CompilerParams(vmem_limit_bytes=16 << 20),
        cost_estimate=pl.CostEstimate(
            flops=LEAD_FLOPS, bytes_accessed=2 * rows * features, transcendentals=0
        ),
        name="prepare",
    )(place, *far)


def fill_rows(half, blocks, refs, own, other, coded):
    tokens = refs[0].shape[0]
    for i in range(blocks):
        rows = slice(i * tokens, (i + 1) * tokens)
        own[rows, :] = refs[i][:, :half]
        other[rows, :] = refs[blocks + i][:, :half]
        coded[rows, :] = refs[i][:, half:].astype(jnp.float32)


def hidden_units(half, experts, place_ref, gate_ref, up_ref, own, other, coded, out_ref):
    local, _, units = gate_ref.shape
    first_slot = place_ref[0] * local
    own_at = pl.ds(pl.multiple_of(place_ref[1] * half, half), half)
    other_at = pl.ds(pl.multiple_of((1 - place_ref[1]) * half, half), half)
    slot = lax.rem(lax.broadcasted_iota(jnp.int32, coded.shape, 1), experts)
    block = min(units, 256)
    for e in range(local):
        weight = jnp.sum(jnp.where(slot == first_slot + e, coded[...], 0.0), axis=1, keepdims=True)
        for at in range(0, units, block):
            cut = slice(at, at + block)

            def project(ref):
                return jnp.dot(
                    own[...], ref[e, own_at, cut], preferred_element_type=jnp.float32
                ) + jnp.dot(other[...], ref[e, other_at, cut], preferred_element_type=jnp.float32)

            gate_act = project(gate_ref)
            up_act = project(up_ref)
            hidden = gate_act / (1.0 + jnp.exp(-gate_act)) * up_act
            hidden = jnp.where(weight > 0.0, hidden * weight, 0.0)
            out_ref[:, e * units + at : e * units + at + block] = hidden.astype(jnp.bfloat16)


def down_copies(down_ref, buffer, sem, at):
    width = buffer.shape[3]
    return [
        pltpu.make_async_copy(
            down_ref.at[:, :, pl.ds(pl.multiple_of(at + j * width, width), width)],
            buffer.at[j],
            sem.at[j],
        )
        for j in range(buffer.shape[0])
    ]


def other_kernel(half, experts, blocks, place_ref, *refs):
    gate_ref, up_ref, down_ref, hidden_ref, send_ref = refs[2 * blocks : 2 * blocks + 5]
    own, other, coded, buffer, sem = refs[2 * blocks + 5 :]
    copies = down_copies(down_ref, buffer, sem, (1 - place_ref[1]) * half)
    for copy in copies:
        copy.start()
    fill_rows(half, blocks, refs, own, other, coded)
    hidden_units(half, experts, place_ref, gate_ref, up_ref, own, other, coded, hidden_ref)
    width = buffer.shape[3]
    for j, copy in enumerate(copies):
        copy.wait()
        total = jnp.dot(
            hidden_ref[...], buffer[j].reshape(-1, width), preferred_element_type=jnp.float32
        )
        send_ref[:, j * width : (j + 1) * width] = total.astype(send_ref.dtype)


def mine_kernel(half, place_ref, hidden_ref, down_ref, *refs):
    out_refs, buffer, sem = refs[:-2], refs[-2], refs[-1]
    copies = down_copies(down_ref, buffer, sem, place_ref[1] * half)
    for copy in copies:
        copy.start()
    width = buffer.shape[3]
    tokens = out_refs[0].shape[0]
    for j, copy in enumerate(copies):
        copy.wait()
        total = jnp.dot(
            hidden_ref[...], buffer[j].reshape(-1, width), preferred_element_type=jnp.float32
        )
        for i, out_ref in enumerate(out_refs):
            out_ref[:, j * width : (j + 1) * width] = total[i * tokens : (i + 1) * tokens]


def run_other(place, own, other, gate, up, down, experts):
    blocks = len(own)
    local, features, width = gate.shape
    rows, half, units = blocks * own[0].shape[0], features // 2, local * width
    vmem, hbm = pl.BlockSpec(memory_space=pltpu.VMEM), pl.BlockSpec(memory_space=pltpu.HBM)
    return pl.pallas_call(
        functools.partial(other_kernel, half, experts, blocks),
        out_shape=[
            jax.ShapeDtypeStruct((rows, units), jnp.bfloat16),
            jax.ShapeDtypeStruct((rows, half), jnp.bfloat16),
        ],
        in_specs=[pl.BlockSpec(memory_space=pltpu.SMEM)] + [vmem] * (2 * blocks + 2) + [hbm],
        out_specs=[vmem] * 2,
        scratch_shapes=[
            pltpu.VMEM((rows, half), jnp.bfloat16),
            pltpu.VMEM((rows, half), jnp.bfloat16),
            pltpu.VMEM((rows, own[0].shape[1] - half), jnp.float32),
            pltpu.VMEM((half // WIDTH, local, width, WIDTH), jnp.bfloat16),
            pltpu.SemaphoreType.DMA((half // WIDTH,)),
        ],
        compiler_params=pltpu.CompilerParams(vmem_limit_bytes=16 << 20),
        cost_estimate=pl.CostEstimate(
            flops=2 * rows * units * (2 * features + half),
            bytes_accessed=4 * rows * half,
            transcendentals=rows * units,
        ),
        name="other",
    )(place, *own, *other, gate, up, down)


def run_mine(place, hidden, down, blocks):
    rows = hidden.shape[0]
    local, width, features = down.shape
    half = features // 2
    vmem, hbm = pl.BlockSpec(memory_space=pltpu.VMEM), pl.BlockSpec(memory_space=pltpu.HBM)
    return pl.pallas_call(
        functools.partial(mine_kernel, half),
        out_shape=[jax.ShapeDtypeStruct((rows // blocks, half), jnp.float32)] * blocks,
        in_specs=[pl.BlockSpec(memory_space=pltpu.SMEM), vmem, hbm],
        out_specs=[vmem] * blocks,
        scratch_shapes=[
            pltpu.VMEM((half // WIDTH, local, width, WIDTH), jnp.bfloat16),
            pltpu.SemaphoreType.DMA((half // WIDTH,)),
        ],
        compiler_params=pltpu.CompilerParams(vmem_limit_bytes=16 << 20),
        cost_estimate=pl.CostEstimate(
            flops=2 * rows * half * hidden.shape[1], bytes_accessed=4 * rows * half, transcendentals=0
        ),
        name="mine",
    )(place, hidden, down)


def on_device(
    hidden_in, expert_ids, route_scores, expert_slot, gate_matrix, up_matrix, down_matrix
):
    token_count, feature_count = hidden_in.shape
    experts = expert_slot.shape[0]
    devices = lax.axis_size("sect")
    half = feature_count // 2
    core = lax.axis_index("tp")
    sect = lax.axis_index("sect")
    inner = 2
    outer = devices // inner

    def along(shift):
        return [
            (o * inner + i, (o + shift) % outer * inner + i)
            for o in range(outer)
            for i in range(inner)
        ]

    across = [(d, d ^ 1) for d in range(devices)]
    cores = [(0, 1), (1, 0)]
    place = jnp.stack([sect, core]).astype(jnp.int32)
    bf16, f32 = jnp.bfloat16, jnp.float32

    packed = prepare(place, hidden_in, expert_ids, route_scores, expert_slot)
    shifts = sorted(range(1, outer), key=lambda k: min(k, outer - k))
    same, opposite = {0: packed}, {}
    for k in shifts:
        same[k] = lax.ppermute(packed, "sect", along(k))
    for k in [0] + shifts:
        opposite[k] = lax.ppermute(same[k], "sect", across)
    down_matrix = pltpu.with_memory_space_constraint(down_matrix, pltpu.HBM)
    near = [same[k] for k in range(outer)]
    far = [opposite[k] for k in range(outer)]
    near_other = [lax.ppermute(block, "tp", cores) for block in near]
    far_other = [lax.ppermute(block, "tp", cores) for block in far]
    hidden, send = run_other(
        place, near + far, near_other + far_other, gate_matrix, up_matrix, down_matrix, experts
    )
    received = lax.ppermute(send, "tp", cores).reshape(inner, outer, token_count, half)
    mine = run_mine(place, hidden, down_matrix, inner * outer)
    near_sum = [mine[k] + received[0, k].astype(f32) for k in range(outer)]
    far_sum = [(mine[outer + k] + received[1, k].astype(f32)).astype(bf16) for k in range(outer)]
    near_sum, far_sum = lax.optimization_barrier((near_sum, far_sum))
    result = lax.dynamic_slice_in_dim(hidden_in, core * half, half, 1).astype(f32)
    order = sorted(range(1, outer), key=lambda k: -min(k, outer - k)) + [0]
    for k in order:
        block = near_sum[k] + lax.ppermute(far_sum[k], "sect", across).astype(f32)
        if k:
            block = lax.ppermute(block.astype(bf16), "sect", along(-k)).astype(f32)
        result = result + block
    return result.astype(bf16)


def solution(mesh):
    placed = (
        P(("groups", "sect"), None),
        P(("groups", "sect"), None),
        P(("groups", "sect"), None),
        P(),
        P("sect", None, "tp"),
        P("sect", None, "tp"),
        P("sect", "tp", None),
    )
    return jax.shard_map(
        on_device,
        mesh=mesh,
        in_specs=placed,
        out_specs=P(("groups", "sect"), "tp"),
        check_vma=False,
    )
```

```python
import functools

import jax
import jax.numpy as jnp
from jax import lax
from jax.experimental import pallas as pl
from jax.experimental.pallas import tpu as pltpu
from jax.sharding import PartitionSpec as P

LANES = 128
WIDTH = 512
LIMIT = 6 << 20
LEAD_FLOPS = 40_000_000_000


def prepare_kernel(half, experts, place_ref, *refs):
    out_ref, slot_ref, hidden_ref, ids_ref, scores_ref, sem = refs[4:]
    copies = [
        pltpu.make_async_copy(refs[i], refs[5 + i], sem.at[i]) for i in range(4)
    ]
    for copy in copies:
        copy.start()
    for copy in copies:
        copy.wait()
    resid = hidden_ref[...].astype(jnp.float32)
    scale = lax.rsqrt(jnp.mean(resid * resid, axis=-1, keepdims=True) + 1e-06)
    own = hidden_ref[:, pl.ds(pl.multiple_of(place_ref[1] * half, half), half)]
    out_ref[:, :half] = (own.astype(jnp.float32) * scale).astype(jnp.bfloat16)
    scores = scores_ref[...]
    mixing = scores / jnp.sum(scores, axis=0, keepdims=True)
    ids = ids_ref[...]
    width = out_ref.shape[1] - half
    row = lax.broadcasted_iota(jnp.int32, (width, 1), 0)
    slot_of_row = lax.rem(row, experts)
    expert_of_row = jnp.zeros((width, 1), jnp.int32)
    for e in range(experts):
        expert_of_row = jnp.where(slot_of_row == slot_ref[e], e, expert_of_row)
    weight = jnp.zeros((width, ids.shape[1]), jnp.float32)
    for k in range(ids.shape[0]):
        weight = weight + jnp.where(ids[k : k + 1, :] == expert_of_row, mixing[k : k + 1, :], 0.0)
    high = weight.astype(jnp.bfloat16).astype(jnp.float32)
    middle = (weight - high).astype(jnp.bfloat16).astype(jnp.float32)
    low = weight - high - middle
    coded = jnp.where(
        row < experts,
        high,
        jnp.where(row < 2 * experts, middle, jnp.where(row < 3 * experts, low, 0.0)),
    )
    out_ref[:, half:] = coded.T.astype(jnp.bfloat16)


def prepare(place, hidden_in, expert_ids, route_scores, expert_slot):
    rows, features = hidden_in.shape
    half = features // 2
    experts = expert_slot.shape[0]
    width = -(-3 * experts // LANES) * LANES
    vmem = pl.BlockSpec(memory_space=pltpu.VMEM)
    smem, hbm = pl.BlockSpec(memory_space=pltpu.SMEM), pl.BlockSpec(memory_space=pltpu.HBM)
    far = [expert_slot, hidden_in, expert_ids.T, route_scores.T]
    far = [pltpu.with_memory_space_constraint(a, pltpu.HBM) for a in far]
    return pl.pallas_call(
        functools.partial(prepare_kernel, half, experts),
        out_shape=jax.ShapeDtypeStruct((rows, half + width), jnp.bfloat16),
        in_specs=[smem, hbm, hbm, hbm, hbm],
        out_specs=vmem,
        scratch_shapes=[
            pltpu.SMEM(expert_slot.shape, jnp.int32),
            pltpu.VMEM(hidden_in.shape, hidden_in.dtype),
            pltpu.VMEM(expert_ids.shape[::-1], jnp.int32),
            pltpu.VMEM(route_scores.shape[::-1], jnp.float32),
            pltpu.SemaphoreType.DMA((4,)),
        ],
        compiler_params=pltpu.CompilerParams(vmem_limit_bytes=LIMIT),
        cost_estimate=pl.CostEstimate(
            flops=LEAD_FLOPS, bytes_accessed=2 * rows * features, transcendentals=0
        ),
        name="prepare",
    )(place, *far)


def fill_rows(half, blocks, refs, own, other, coded):
    tokens = refs[0].shape[0]
    for i in range(blocks):
        rows = slice(i * tokens, (i + 1) * tokens)
        own[rows, :] = refs[i][:, :half]
        other[rows, :] = refs[blocks + i][:, :half]
        coded[rows, :] = refs[i][:, half:].astype(jnp.float32)


def hidden_units(half, experts, place_ref, gate_ref, up_ref, own, other, coded, out_ref):
    local, _, units = gate_ref.shape
    first_slot = place_ref[0] * local
    own_at = pl.ds(pl.multiple_of(place_ref[1] * half, half), half)
    other_at = pl.ds(pl.multiple_of((1 - place_ref[1]) * half, half), half)
    slot = lax.rem(lax.broadcasted_iota(jnp.int32, coded.shape, 1), experts)
    block = min(units, 256)
    for e in range(local):
        weight = jnp.sum(jnp.where(slot == first_slot + e, coded[...], 0.0), axis=1, keepdims=True)
        for at in range(0, units, block):
            cut = slice(at, at + block)

            def project(ref):
                return jnp.dot(
                    own[...], ref[e, own_at, cut], preferred_element_type=jnp.float32
                ) + jnp.dot(other[...], ref[e, other_at, cut], preferred_element_type=jnp.float32)

            gate_act = project(gate_ref)
            up_act = project(up_ref)
            hidden = gate_act / (1.0 + jnp.exp(-gate_act)) * up_act
            hidden = jnp.where(weight > 0.0, hidden * weight, 0.0)
            out_ref[:, e * units + at : e * units + at + block] = hidden.astype(jnp.bfloat16)


def hidden_kernel(half, experts, blocks, place_ref, *refs):
    gate_ref, up_ref, out_ref, own, other, coded = refs[2 * blocks :]
    fill_rows(half, blocks, refs, own, other, coded)
    hidden_units(half, experts, place_ref, gate_ref, up_ref, own, other, coded, out_ref)


def run_hidden(place, own, other, gate, up, experts):
    blocks = len(own)
    local, features, width = gate.shape
    rows, half, units = blocks * own[0].shape[0], features // 2, local * width
    vmem = pl.BlockSpec(memory_space=pltpu.VMEM)
    return pl.pallas_call(
        functools.partial(hidden_kernel, half, experts, blocks),
        out_shape=jax.ShapeDtypeStruct((rows, units), jnp.bfloat16),
        in_specs=[pl.BlockSpec(memory_space=pltpu.SMEM)] + [vmem] * (2 * blocks + 2),
        out_specs=vmem,
        scratch_shapes=[
            pltpu.VMEM((rows, half), jnp.bfloat16),
            pltpu.VMEM((rows, half), jnp.bfloat16),
            pltpu.VMEM((rows, own[0].shape[1] - half), jnp.float32),
        ],
        compiler_params=pltpu.CompilerParams(vmem_limit_bytes=LIMIT),
        cost_estimate=pl.CostEstimate(
            flops=4 * rows * units * features, bytes_accessed=4 * rows * half, transcendentals=rows * units
        ),
        name="hidden",
    )(place, *own, *other, gate, up)


def down_kernel(mine, far, place_ref, hidden_ref, down_ref, *refs):
    out_refs = refs[mine:]
    local, units, features = down_ref.shape
    half = features // 2
    core = place_ref[1] if mine else 1 - place_ref[1]
    rows = hidden_ref.shape[0] // 2
    tokens = out_refs[0].shape[0]
    hidden = hidden_ref[far * rows : (far + 1) * rows, :]
    for at in range(0, half, WIDTH):
        cut = pl.ds(pl.multiple_of(core * half + at, WIDTH), WIDTH)
        total = jnp.dot(
            hidden,
            down_ref[:, :, cut].reshape(local * units, WIDTH),
            preferred_element_type=jnp.float32,
        )
        if mine:
            total = total + refs[0][:, at : at + WIDTH].astype(jnp.float32)
        for i, out_ref in enumerate(out_refs):
            out_ref[:, at : at + WIDTH] = total[i * tokens : (i + 1) * tokens].astype(out_ref.dtype)


def run_down(place, hidden, down, far, received, kind, blocks):
    rows, half = hidden.shape[0] // 2, down.shape[2] // 2
    vmem = pl.BlockSpec(memory_space=pltpu.VMEM)
    extra = [] if received is None else [received]
    return pl.pallas_call(
        functools.partial(down_kernel, len(extra), far),
        out_shape=[jax.ShapeDtypeStruct((rows // blocks, half), kind)] * blocks,
        in_specs=[pl.BlockSpec(memory_space=pltpu.SMEM)] + [vmem] * (2 + len(extra)),
        out_specs=[vmem] * blocks,
        compiler_params=pltpu.CompilerParams(vmem_limit_bytes=LIMIT),
        cost_estimate=pl.CostEstimate(
            flops=2 * rows * half * hidden.shape[1], bytes_accessed=4 * rows * half, transcendentals=0
        ),
        name="mine" if extra else "other",
    )(place, hidden, down, *extra)


def on_device(
    hidden_in, expert_ids, route_scores, expert_slot, gate_matrix, up_matrix, down_matrix
):
    token_count, feature_count = hidden_in.shape
    experts = expert_slot.shape[0]
    devices = lax.axis_size("sect")
    half = feature_count // 2
    core = lax.axis_index("tp")
    sect = lax.axis_index("sect")
    inner = 2
    outer = devices // inner

    def along(shift):
        return [
            (o * inner + i, (o + shift) % outer * inner + i)
            for o in range(outer)
            for i in range(inner)
        ]

    across = [(d, d ^ 1) for d in range(devices)]
    cores = [(0, 1), (1, 0)]
    place = jnp.stack([sect, core]).astype(jnp.int32)
    bf16, f32 = jnp.bfloat16, jnp.float32

    packed = prepare(place, hidden_in, expert_ids, route_scores, expert_slot)
    shifts = sorted(range(1, outer), key=lambda k: min(k, outer - k))
    same, opposite = {0: packed}, {}
    for k in shifts:
        same[k] = lax.ppermute(packed, "sect", along(k))
    for k in [0] + shifts:
        opposite[k] = lax.ppermute(same[k], "sect", across)
    near = [same[k] for k in range(outer)]
    far = [opposite[k] for k in range(outer)]
    near_other = [lax.ppermute(block, "tp", cores) for block in near]
    far_other = [lax.ppermute(block, "tp", cores) for block in far]
    hidden = run_hidden(place, near + far, near_other + far_other, gate_matrix, up_matrix, experts)
    far_send = lax.ppermute(run_down(place, hidden, down_matrix, 1, None, bf16, 1)[0], "tp", cores)
    near_send = lax.ppermute(run_down(place, hidden, down_matrix, 0, None, bf16, 1)[0], "tp", cores)
    far_sum = run_down(place, hidden, down_matrix, 1, far_send, bf16, outer)
    near_sum = run_down(place, hidden, down_matrix, 0, near_send, f32, outer)
    result = lax.dynamic_slice_in_dim(hidden_in, core * half, half, 1).astype(f32)
    order = sorted(range(1, outer), key=lambda k: -min(k, outer - k)) + [0]
    for k in order:
        block = near_sum[k] + lax.ppermute(far_sum[k], "sect", across).astype(f32)
        if k:
            block = lax.ppermute(block.astype(bf16), "sect", along(-k)).astype(f32)
        result = result + block
    return result.astype(bf16)


def solution(mesh):
    placed = (
        P(("groups", "sect"), None),
        P(("groups", "sect"), None),
        P(("groups", "sect"), None),
        P(),
        P("sect", None, "tp"),
        P("sect", None, "tp"),
        P("sect", "tp", None),
    )
    return jax.shard_map(
        on_device,
        mesh=mesh,
        in_specs=placed,
        out_specs=P(("groups", "sect"), "tp"),
        check_vma=False,
    )
```

```python
import functools

import jax
import jax.numpy as jnp
from jax import lax
from jax.experimental import pallas as pl
from jax.experimental.pallas import tpu as pltpu
from jax.sharding import PartitionSpec as P

LANES = 128
WIDTH = 512
LIMIT = 6 << 20
LEAD_FLOPS = 40_000_000_000


def prepare_kernel(half, experts, place_ref, *refs):
    out_ref, slot_ref, hidden_ref, ids_ref, scores_ref, sem = refs[4:]
    copies = [
        pltpu.make_async_copy(refs[i], refs[5 + i], sem.at[i]) for i in range(4)
    ]
    for copy in copies:
        copy.start()
    for copy in copies:
        copy.wait()
    resid = hidden_ref[...].astype(jnp.float32)
    scale = lax.rsqrt(jnp.mean(resid * resid, axis=-1, keepdims=True) + 1e-06)
    own = hidden_ref[:, pl.ds(pl.multiple_of(place_ref[1] * half, half), half)]
    out_ref[:, :half] = (own.astype(jnp.float32) * scale).astype(jnp.bfloat16)
    scores = scores_ref[...]
    mixing = scores / jnp.sum(scores, axis=0, keepdims=True)
    ids = ids_ref[...]
    width = out_ref.shape[1] - half
    row = lax.broadcasted_iota(jnp.int32, (width, 1), 0)
    slot_of_row = lax.rem(row, experts)
    expert_of_row = jnp.zeros((width, 1), jnp.int32)
    for e in range(experts):
        expert_of_row = jnp.where(slot_of_row == slot_ref[e], e, expert_of_row)
    weight = jnp.zeros((width, ids.shape[1]), jnp.float32)
    for k in range(ids.shape[0]):
        weight = weight + jnp.where(ids[k : k + 1, :] == expert_of_row, mixing[k : k + 1, :], 0.0)
    high = weight.astype(jnp.bfloat16).astype(jnp.float32)
    middle = (weight - high).astype(jnp.bfloat16).astype(jnp.float32)
    low = weight - high - middle
    coded = jnp.where(
        row < experts,
        high,
        jnp.where(row < 2 * experts, middle, jnp.where(row < 3 * experts, low, 0.0)),
    )
    out_ref[:, half:] = coded.T.astype(jnp.bfloat16)


def prepare(place, hidden_in, expert_ids, route_scores, expert_slot):
    rows, features = hidden_in.shape
    half = features // 2
    experts = expert_slot.shape[0]
    width = -(-3 * experts // LANES) * LANES
    vmem = pl.BlockSpec(memory_space=pltpu.VMEM)
    smem, hbm = pl.BlockSpec(memory_space=pltpu.SMEM), pl.BlockSpec(memory_space=pltpu.HBM)
    far = [expert_slot, hidden_in, expert_ids.T, route_scores.T]
    far = [pltpu.with_memory_space_constraint(a, pltpu.HBM) for a in far]
    return pl.pallas_call(
        functools.partial(prepare_kernel, half, experts),
        out_shape=jax.ShapeDtypeStruct((rows, half + width), jnp.bfloat16),
        in_specs=[smem, hbm, hbm, hbm, hbm],
        out_specs=vmem,
        scratch_shapes=[
            pltpu.SMEM(expert_slot.shape, jnp.int32),
            pltpu.VMEM(hidden_in.shape, hidden_in.dtype),
            pltpu.VMEM(expert_ids.shape[::-1], jnp.int32),
            pltpu.VMEM(route_scores.shape[::-1], jnp.float32),
            pltpu.SemaphoreType.DMA((4,)),
        ],
        compiler_params=pltpu.CompilerParams(vmem_limit_bytes=LIMIT),
        cost_estimate=pl.CostEstimate(
            flops=LEAD_FLOPS, bytes_accessed=2 * rows * features, transcendentals=0
        ),
        name="prepare",
    )(place, *far)


def fill_rows(half, blocks, refs, own, other, coded):
    tokens = refs[0].shape[0]
    for i in range(blocks):
        rows = slice(i * tokens, (i + 1) * tokens)
        own[rows, :] = refs[i][:, :half]
        other[rows, :] = refs[blocks + i][:, :half]
        coded[rows, :] = refs[i][:, half:].astype(jnp.float32)


def hidden_units(half, experts, place_ref, gate_ref, up_ref, own, other, coded, out_refs):
    local, _, units = gate_ref.shape
    first_slot = place_ref[0] * local
    own_at = pl.ds(pl.multiple_of(place_ref[1] * half, half), half)
    other_at = pl.ds(pl.multiple_of((1 - place_ref[1]) * half, half), half)
    slot = lax.rem(lax.broadcasted_iota(jnp.int32, coded.shape, 1), experts)
    block = min(units, 256)
    for e in range(local):
        weight = jnp.sum(jnp.where(slot == first_slot + e, coded[...], 0.0), axis=1, keepdims=True)
        for at in range(0, units, block):
            cut = slice(at, at + block)

            def project(ref):
                return jnp.dot(
                    own[...], ref[e, own_at, cut], preferred_element_type=jnp.float32
                ) + jnp.dot(other[...], ref[e, other_at, cut], preferred_element_type=jnp.float32)

            gate_act = project(gate_ref)
            up_act = project(up_ref)
            hidden = gate_act / (1.0 + jnp.exp(-gate_act)) * up_act
            hidden = jnp.where(weight > 0.0, hidden * weight, 0.0)
            columns = slice(e * units + at, e * units + at + block)
            for i, out_ref in enumerate(out_refs):
                rows = out_ref.shape[0]
                out_ref[:, columns] = hidden[i * rows : (i + 1) * rows].astype(jnp.bfloat16)


def hidden_kernel(half, experts, blocks, place_ref, *refs):
    gate_ref, up_ref, *out_refs = refs[2 * blocks : 2 * blocks + 4]
    own, other, coded = refs[2 * blocks + 4 :]
    fill_rows(half, blocks, refs, own, other, coded)
    hidden_units(half, experts, place_ref, gate_ref, up_ref, own, other, coded, out_refs)


def run_hidden(place, own, other, gate, up, experts):
    blocks = len(own)
    local, features, width = gate.shape
    rows, half, units = blocks * own[0].shape[0], features // 2, local * width
    vmem = pl.BlockSpec(memory_space=pltpu.VMEM)
    return pl.pallas_call(
        functools.partial(hidden_kernel, half, experts, blocks),
        out_shape=[jax.ShapeDtypeStruct((rows // 2, units), jnp.bfloat16)] * 2,
        in_specs=[pl.BlockSpec(memory_space=pltpu.SMEM)] + [vmem] * (2 * blocks + 2),
        out_specs=[vmem] * 2,
        scratch_shapes=[
            pltpu.VMEM((rows, half), jnp.bfloat16),
            pltpu.VMEM((rows, half), jnp.bfloat16),
            pltpu.VMEM((rows, own[0].shape[1] - half), jnp.float32),
        ],
        compiler_params=pltpu.CompilerParams(vmem_limit_bytes=LIMIT),
        cost_estimate=pl.CostEstimate(
            flops=4 * rows * units * features, bytes_accessed=4 * rows * half, transcendentals=rows * units
        ),
        name="hidden",
    )(place, *own, *other, gate, up)


def down_kernel(mine, place_ref, hidden_ref, down_ref, *refs):
    out_refs = refs[mine:]
    local, units, features = down_ref.shape
    half = features // 2
    core = place_ref[1] if mine else 1 - place_ref[1]
    tokens = out_refs[0].shape[0]
    for at in range(0, half, WIDTH):
        cut = pl.ds(pl.multiple_of(core * half + at, WIDTH), WIDTH)
        total = jnp.dot(
            hidden_ref[...],
            down_ref[:, :, cut].reshape(local * units, WIDTH),
            preferred_element_type=jnp.float32,
        )
        if mine:
            total = total + refs[0][:, at : at + WIDTH].astype(jnp.float32)
        for i, out_ref in enumerate(out_refs):
            out_ref[:, at : at + WIDTH] = total[i * tokens : (i + 1) * tokens].astype(out_ref.dtype)


def run_down(place, hidden, down, received, kinds):
    rows, half = hidden.shape[0], down.shape[2] // 2
    vmem = pl.BlockSpec(memory_space=pltpu.VMEM)
    extra = [] if received is None else [received]
    return pl.pallas_call(
        functools.partial(down_kernel, len(extra)),
        out_shape=[jax.ShapeDtypeStruct((rows // len(kinds), half), kind) for kind in kinds],
        in_specs=[pl.BlockSpec(memory_space=pltpu.SMEM)] + [vmem] * (2 + len(extra)),
        out_specs=[vmem] * len(kinds),
        compiler_params=pltpu.CompilerParams(vmem_limit_bytes=LIMIT),
        cost_estimate=pl.CostEstimate(
            flops=2 * rows * half * hidden.shape[1], bytes_accessed=4 * rows * half, transcendentals=0
        ),
        name="mine" if extra else "other",
    )(place, hidden, down, *extra)


def after(value, *others):
    return lax.optimization_barrier((value, *others))[0]


def on_device(
    hidden_in, expert_ids, route_scores, expert_slot, gate_matrix, up_matrix, down_matrix
):
    token_count, feature_count = hidden_in.shape
    experts = expert_slot.shape[0]
    devices = lax.axis_size("sect")
    half = feature_count // 2
    core = lax.axis_index("tp")
    sect = lax.axis_index("sect")
    inner = 2
    outer = devices // inner

    def along(shift):
        return [
            (o * inner + i, (o + shift) % outer * inner + i)
            for o in range(outer)
            for i in range(inner)
        ]

    across = [(d, d ^ 1) for d in range(devices)]
    cores = [(0, 1), (1, 0)]
    place = jnp.stack([sect, core]).astype(jnp.int32)
    bf16, f32 = jnp.bfloat16, jnp.float32

    packed = prepare(place, hidden_in, expert_ids, route_scores, expert_slot)
    turned = 1
    order = sorted(range(1, outer), key=lambda k: -min(k, outer - k))
    same, opposite = {0: packed}, {0: lax.ppermute(packed, "sect", across)}
    for k in order:
        if k != turned:
            same[k] = lax.ppermute(packed, "sect", along(k))
    if turned < outer:
        same[turned] = lax.ppermute(after(packed, opposite[0]), "sect", along(turned))
        opposite[turned] = lax.ppermute(opposite[0], "sect", along(turned))
    for k in order[::-1]:
        if k != turned:
            block = same[k]
            if k == order[0]:
                block = after(block, same[turned], opposite[turned])
            opposite[k] = lax.ppermute(block, "sect", across)
    near = [same[k] for k in range(outer)]
    far = [opposite[k] for k in range(outer)]
    near_other = [lax.ppermute(block, "tp", cores) for block in near]
    far_other = [lax.ppermute(block, "tp", cores) for block in far]
    near, far = run_hidden(
        place, near + far, near_other + far_other, gate_matrix, up_matrix, experts
    )
    far_send = lax.ppermute(run_down(place, far, down_matrix, None, [bf16])[0], "tp", cores)
    near_send = lax.ppermute(run_down(place, near, down_matrix, None, [bf16])[0], "tp", cores)
    kinds = [f32] + [bf16] * (outer - 1)
    far_sum = list(run_down(place, far, down_matrix, far_send, kinds))
    kinds = [bf16 if k == turned else f32 for k in range(outer)]
    near_sum = run_down(place, near, down_matrix, near_send, kinds)
    result = lax.dynamic_slice_in_dim(hidden_in, core * half, half, 1).astype(f32)
    if turned < outer:
        gone = lax.ppermute(far_sum[turned], "sect", along(-turned)).astype(f32)
        far_sum[0] = (far_sum[0] + gone).astype(bf16)
        result = result + lax.ppermute(near_sum[turned], "sect", along(-turned)).astype(f32)
    for k in [k for k in order if k != turned] + [0]:
        crossed = lax.ppermute(far_sum[k].astype(bf16), "sect", across).astype(f32)
        block = near_sum[k] + crossed
        if k:
            block = lax.ppermute(block.astype(bf16), "sect", along(-k)).astype(f32)
        result = result + block
    return result.astype(bf16)


def solution(mesh):
    placed = (
        P(("groups", "sect"), None),
        P(("groups", "sect"), None),
        P(("groups", "sect"), None),
        P(),
        P("sect", None, "tp"),
        P("sect", None, "tp"),
        P("sect", "tp", None),
    )
    return jax.shard_map(
        on_device,
        mesh=mesh,
        in_specs=placed,
        out_specs=P(("groups", "sect"), "tp"),
        check_vma=False,
    )
```

```python
import functools

import jax
import jax.numpy as jnp
from jax import lax
from jax.experimental import pallas as pl
from jax.experimental.pallas import tpu as pltpu
from jax.sharding import PartitionSpec as P

LANES = 128
WIDTH = 512
LIMIT = 6 << 20
LEAD_FLOPS = 40_000_000_000


def prepare_kernel(half, experts, place_ref, *refs):
    out_ref, slot_ref, hidden_ref, ids_ref, scores_ref, sem = refs[4:]
    copies = [
        pltpu.make_async_copy(refs[i], refs[5 + i], sem.at[i]) for i in range(4)
    ]
    for copy in copies:
        copy.start()
    for copy in copies:
        copy.wait()
    resid = hidden_ref[...].astype(jnp.float32)
    scale = lax.rsqrt(jnp.mean(resid * resid, axis=-1, keepdims=True) + 1e-06)
    own = hidden_ref[:, pl.ds(pl.multiple_of(place_ref[1] * half, half), half)]
    out_ref[:, :half] = (own.astype(jnp.float32) * scale).astype(jnp.bfloat16)
    scores = scores_ref[...]
    mixing = scores / jnp.sum(scores, axis=0, keepdims=True)
    ids = ids_ref[...]
    width = out_ref.shape[1] - half
    row = lax.broadcasted_iota(jnp.int32, (width, 1), 0)
    slot_of_row = lax.rem(row, experts)
    expert_of_row = jnp.zeros((width, 1), jnp.int32)
    for e in range(experts):
        expert_of_row = jnp.where(slot_of_row == slot_ref[e], e, expert_of_row)
    weight = jnp.zeros((width, ids.shape[1]), jnp.float32)
    for k in range(ids.shape[0]):
        weight = weight + jnp.where(ids[k : k + 1, :] == expert_of_row, mixing[k : k + 1, :], 0.0)
    high = weight.astype(jnp.bfloat16).astype(jnp.float32)
    middle = (weight - high).astype(jnp.bfloat16).astype(jnp.float32)
    low = weight - high - middle
    coded = jnp.where(
        row < experts,
        high,
        jnp.where(row < 2 * experts, middle, jnp.where(row < 3 * experts, low, 0.0)),
    )
    out_ref[:, half:] = coded.T.astype(jnp.bfloat16)


def prepare(place, hidden_in, expert_ids, route_scores, expert_slot):
    rows, features = hidden_in.shape
    half = features // 2
    experts = expert_slot.shape[0]
    width = -(-3 * experts // LANES) * LANES
    vmem = pl.BlockSpec(memory_space=pltpu.VMEM)
    smem, hbm = pl.BlockSpec(memory_space=pltpu.SMEM), pl.BlockSpec(memory_space=pltpu.HBM)
    far = [expert_slot, hidden_in, expert_ids.T, route_scores.T]
    far = [pltpu.with_memory_space_constraint(a, pltpu.HBM) for a in far]
    return pl.pallas_call(
        functools.partial(prepare_kernel, half, experts),
        out_shape=jax.ShapeDtypeStruct((rows, half + width), jnp.bfloat16),
        in_specs=[smem, hbm, hbm, hbm, hbm],
        out_specs=vmem,
        scratch_shapes=[
            pltpu.SMEM(expert_slot.shape, jnp.int32),
            pltpu.VMEM(hidden_in.shape, hidden_in.dtype),
            pltpu.VMEM(expert_ids.shape[::-1], jnp.int32),
            pltpu.VMEM(route_scores.shape[::-1], jnp.float32),
            pltpu.SemaphoreType.DMA((4,)),
        ],
        compiler_params=pltpu.CompilerParams(vmem_limit_bytes=LIMIT),
        cost_estimate=pl.CostEstimate(
            flops=LEAD_FLOPS, bytes_accessed=2 * rows * features, transcendentals=0
        ),
        name="prepare",
    )(place, *far)


def fill_rows(half, blocks, refs, own, other, coded):
    tokens = refs[0].shape[0]
    for i in range(blocks):
        rows = slice(i * tokens, (i + 1) * tokens)
        own[rows, :] = refs[i][:, :half]
        other[rows, :] = refs[blocks + i][:, :half]
        coded[rows, :] = refs[i][:, half:].astype(jnp.float32)


def hidden_units(half, experts, place_ref, gate_ref, up_ref, own, other, coded, out_refs):
    local, _, units = gate_ref.shape
    first_slot = place_ref[0] * local
    own_at = pl.ds(pl.multiple_of(place_ref[1] * half, half), half)
    other_at = pl.ds(pl.multiple_of((1 - place_ref[1]) * half, half), half)
    slot = lax.rem(lax.broadcasted_iota(jnp.int32, coded.shape, 1), experts)
    block = min(units, 256)
    for e in range(local):
        weight = jnp.sum(jnp.where(slot == first_slot + e, coded[...], 0.0), axis=1, keepdims=True)
        for at in range(0, units, block):
            cut = slice(at, at + block)

            def project(ref):
                return jnp.dot(
                    own[...], ref[e, own_at, cut], preferred_element_type=jnp.float32
                ) + jnp.dot(other[...], ref[e, other_at, cut], preferred_element_type=jnp.float32)

            gate_act = project(gate_ref)
            up_act = project(up_ref)
            hidden = gate_act / (1.0 + jnp.exp(-gate_act)) * up_act
            hidden = jnp.where(weight > 0.0, hidden * weight, 0.0)
            columns = slice(e * units + at, e * units + at + block)
            row = 0
            for out_ref in out_refs:
                rows = slice(row, row + out_ref.shape[0])
                out_ref[:, columns] = hidden[rows].astype(jnp.bfloat16)
                row += out_ref.shape[0]


def hidden_kernel(half, experts, blocks, place_ref, *refs):
    gate_ref, up_ref, *out_refs = refs[2 * blocks : 2 * blocks + 4]
    own, other, coded = refs[2 * blocks + 4 :]
    fill_rows(half, blocks, refs, own, other, coded)
    hidden_units(half, experts, place_ref, gate_ref, up_ref, own, other, coded, out_refs)


def run_hidden(place, own, other, gate, up, experts, first):
    blocks = len(own)
    local, features, width = gate.shape
    rows, half, units = blocks * own[0].shape[0], features // 2, local * width
    vmem = pl.BlockSpec(memory_space=pltpu.VMEM)
    return pl.pallas_call(
        functools.partial(hidden_kernel, half, experts, blocks),
        out_shape=[
            jax.ShapeDtypeStruct((count * own[0].shape[0], units), jnp.bfloat16)
            for count in (first, blocks - first)
        ],
        in_specs=[pl.BlockSpec(memory_space=pltpu.SMEM)] + [vmem] * (2 * blocks + 2),
        out_specs=[vmem] * 2,
        scratch_shapes=[
            pltpu.VMEM((rows, half), jnp.bfloat16),
            pltpu.VMEM((rows, half), jnp.bfloat16),
            pltpu.VMEM((rows, own[0].shape[1] - half), jnp.float32),
        ],
        compiler_params=pltpu.CompilerParams(vmem_limit_bytes=LIMIT),
        cost_estimate=pl.CostEstimate(
            flops=4 * rows * units * features, bytes_accessed=4 * rows * half, transcendentals=rows * units
        ),
        name="hidden",
    )(place, *own, *other, gate, up)


def down_kernel(mine, place_ref, hidden_ref, down_ref, *refs):
    out_refs = refs[mine:]
    local, units, features = down_ref.shape
    half = features // 2
    core = place_ref[1] if mine else 1 - place_ref[1]
    tokens = out_refs[0].shape[0]
    for at in range(0, half, WIDTH):
        cut = pl.ds(pl.multiple_of(core * half + at, WIDTH), WIDTH)
        total = jnp.dot(
            hidden_ref[...],
            down_ref[:, :, cut].reshape(local * units, WIDTH),
            preferred_element_type=jnp.float32,
        )
        if mine:
            total = total + refs[0][:, at : at + WIDTH].astype(jnp.float32)
        for i, out_ref in enumerate(out_refs):
            out_ref[:, at : at + WIDTH] = total[i * tokens : (i + 1) * tokens].astype(out_ref.dtype)


def run_down(place, hidden, down, received, kinds):
    rows, half = hidden.shape[0], down.shape[2] // 2
    vmem = pl.BlockSpec(memory_space=pltpu.VMEM)
    extra = [] if received is None else [received]
    return pl.pallas_call(
        functools.partial(down_kernel, len(extra)),
        out_shape=[jax.ShapeDtypeStruct((rows // len(kinds), half), kind) for kind in kinds],
        in_specs=[pl.BlockSpec(memory_space=pltpu.SMEM)] + [vmem] * (2 + len(extra)),
        out_specs=[vmem] * len(kinds),
        compiler_params=pltpu.CompilerParams(vmem_limit_bytes=LIMIT),
        cost_estimate=pl.CostEstimate(
            flops=2 * rows * half, bytes_accessed=4 * rows, transcendentals=0
        ),
        name="mine" if extra else "other",
    )(place, hidden, down, *extra)


def after(value, *others):
    return lax.optimization_barrier((value, *others))[0]


def on_device(
    hidden_in, expert_ids, route_scores, expert_slot, gate_matrix, up_matrix, down_matrix
):
    token_count, feature_count = hidden_in.shape
    experts = expert_slot.shape[0]
    devices = lax.axis_size("sect")
    half = feature_count // 2
    core = lax.axis_index("tp")
    sect = lax.axis_index("sect")
    inner = 2
    outer = devices // inner

    def along(shift):
        return [
            (o * inner + i, (o + shift) % outer * inner + i)
            for o in range(outer)
            for i in range(inner)
        ]

    across = [(d, d ^ 1) for d in range(devices)]
    cores = [(0, 1), (1, 0)]
    place = jnp.stack([sect, core]).astype(jnp.int32)
    bf16, f32 = jnp.bfloat16, jnp.float32

    packed = prepare(place, hidden_in, expert_ids, route_scores, expert_slot)
    turned = 1
    order = sorted(range(1, outer), key=lambda k: -min(k, outer - k))
    same, opposite = {0: packed}, {0: lax.ppermute(packed, "sect", across)}
    for k in order[::-1]:
        block = after(packed, opposite[0]) if k == order[0] and outer > 2 else packed
        same[k] = lax.ppermute(block, "sect", along(k))
    for k in order[::-1]:
        opposite[k] = lax.ppermute(same[k], "sect", across)
    early = [(opposite, k) for k in range(outer)] + [(same, k) for k in range(outer) if k == turned]
    late = [(same, k) for k in range(outer) if k != turned]
    blocks = [side[k] for side, k in early + late]
    others = [lax.ppermute(block, "tp", cores) for block in blocks]
    groups = run_hidden(place, blocks, others, gate_matrix, up_matrix, experts, len(early))
    sent = [
        lax.ppermute(run_down(place, hidden, down_matrix, None, [bf16])[0], "tp", cores)
        for hidden in groups
    ]
    far_sum, near_sum = {}, {}
    for group, hidden, received in zip((early, late), groups, sent):
        kinds = [
            bf16 if k == turned or (side is opposite and k) else f32 for side, k in group
        ]
        sums = run_down(place, hidden, down_matrix, received, kinds)
        for (side, k), total in zip(group, sums):
            (far_sum if side is opposite else near_sum)[k] = total
    result = lax.dynamic_slice_in_dim(hidden_in, core * half, half, 1).astype(f32)
    if turned < outer:
        gone = lax.ppermute(far_sum[turned], "sect", along(-turned)).astype(f32)
        far_sum[0] = (far_sum[0] + gone).astype(bf16)
        result = result + lax.ppermute(near_sum[turned], "sect", along(-turned)).astype(f32)
    for k in [k for k in order if k != turned] + [0]:
        crossed = lax.ppermute(far_sum[k].astype(bf16), "sect", across).astype(f32)
        block = near_sum[k] + crossed
        if k:
            block = lax.ppermute(block.astype(bf16), "sect", along(-k)).astype(f32)
        result = result + block
    return result.astype(bf16)


def solution(mesh):
    placed = (
        P(("groups", "sect"), None),
        P(("groups", "sect"), None),
        P(("groups", "sect"), None),
        P(),
        P("sect", None, "tp"),
        P("sect", None, "tp"),
        P("sect", "tp", None),
    )
    return jax.shard_map(
        on_device,
        mesh=mesh,
        in_specs=placed,
        out_specs=P(("groups", "sect"), "tp"),
        check_vma=False,
    )
```

```python
import functools

import jax
import jax.numpy as jnp
from jax import lax
from jax.experimental import pallas as pl
from jax.experimental.pallas import tpu as pltpu
from jax.sharding import PartitionSpec as P

LANES = 128
WIDTH = 512
LIMIT = 6 << 20
LEAD_FLOPS = 40_000_000_000


def prepare_kernel(half, experts, place_ref, *refs):
    out_ref, slot_ref, hidden_ref, ids_ref, scores_ref, sem = refs[4:]
    copies = [
        pltpu.make_async_copy(refs[i], refs[5 + i], sem.at[i]) for i in range(4)
    ]
    for copy in copies:
        copy.start()
    for copy in copies:
        copy.wait()
    resid = hidden_ref[...].astype(jnp.float32)
    scale = lax.rsqrt(jnp.mean(resid * resid, axis=-1, keepdims=True) + 1e-06)
    own = hidden_ref[:, pl.ds(pl.multiple_of(place_ref[1] * half, half), half)]
    out_ref[:, :half] = (own.astype(jnp.float32) * scale).astype(jnp.bfloat16)
    scores = scores_ref[...]
    mixing = scores / jnp.sum(scores, axis=0, keepdims=True)
    ids = ids_ref[...]
    width = out_ref.shape[1] - half
    row = lax.broadcasted_iota(jnp.int32, (width, 1), 0)
    slot_of_row = lax.rem(row, experts)
    expert_of_row = jnp.zeros((width, 1), jnp.int32)
    for e in range(experts):
        expert_of_row = jnp.where(slot_of_row == slot_ref[e], e, expert_of_row)
    weight = jnp.zeros((width, ids.shape[1]), jnp.float32)
    for k in range(ids.shape[0]):
        weight = weight + jnp.where(ids[k : k + 1, :] == expert_of_row, mixing[k : k + 1, :], 0.0)
    high = weight.astype(jnp.bfloat16).astype(jnp.float32)
    middle = (weight - high).astype(jnp.bfloat16).astype(jnp.float32)
    low = weight - high - middle
    coded = jnp.where(
        row < experts,
        high,
        jnp.where(row < 2 * experts, middle, jnp.where(row < 3 * experts, low, 0.0)),
    )
    out_ref[:, half:] = coded.T.astype(jnp.bfloat16)


def prepare(place, hidden_in, expert_ids, route_scores, expert_slot):
    rows, features = hidden_in.shape
    half = features // 2
    experts = expert_slot.shape[0]
    width = -(-3 * experts // LANES) * LANES
    vmem = pl.BlockSpec(memory_space=pltpu.VMEM)
    smem, hbm = pl.BlockSpec(memory_space=pltpu.SMEM), pl.BlockSpec(memory_space=pltpu.HBM)
    far = [expert_slot, hidden_in, expert_ids.T, route_scores.T]
    far = [pltpu.with_memory_space_constraint(a, pltpu.HBM) for a in far]
    return pl.pallas_call(
        functools.partial(prepare_kernel, half, experts),
        out_shape=jax.ShapeDtypeStruct((rows, half + width), jnp.bfloat16),
        in_specs=[smem, hbm, hbm, hbm, hbm],
        out_specs=vmem,
        scratch_shapes=[
            pltpu.SMEM(expert_slot.shape, jnp.int32),
            pltpu.VMEM(hidden_in.shape, hidden_in.dtype),
            pltpu.VMEM(expert_ids.shape[::-1], jnp.int32),
            pltpu.VMEM(route_scores.shape[::-1], jnp.float32),
            pltpu.SemaphoreType.DMA((4,)),
        ],
        compiler_params=pltpu.CompilerParams(vmem_limit_bytes=LIMIT),
        cost_estimate=pl.CostEstimate(
            flops=LEAD_FLOPS, bytes_accessed=2 * rows * features, transcendentals=0
        ),
        name="prepare",
    )(place, *far)


def fill_rows(half, blocks, refs, own, other, coded):
    tokens = refs[0].shape[0]
    for i in range(blocks):
        rows = slice(i * tokens, (i + 1) * tokens)
        own[rows, :] = refs[i][:, :half]
        other[rows, :] = refs[blocks + i][:, :half]
        coded[rows, :] = refs[i][:, half:].astype(jnp.float32)


def hidden_units(half, experts, place_ref, gate_ref, up_ref, own, other, coded, out_refs):
    local, _, units = gate_ref.shape
    first_slot = place_ref[0] * local
    own_at = pl.ds(pl.multiple_of(place_ref[1] * half, half), half)
    other_at = pl.ds(pl.multiple_of((1 - place_ref[1]) * half, half), half)
    slot = lax.rem(lax.broadcasted_iota(jnp.int32, coded.shape, 1), experts)
    block = min(units, 256)
    for e in range(local):
        weight = jnp.sum(jnp.where(slot == first_slot + e, coded[...], 0.0), axis=1, keepdims=True)
        for at in range(0, units, block):
            cut = slice(at, at + block)

            def project(ref):
                return jnp.dot(
                    own[...], ref[e, own_at, cut], preferred_element_type=jnp.float32
                ) + jnp.dot(other[...], ref[e, other_at, cut], preferred_element_type=jnp.float32)

            gate_act = project(gate_ref)
            up_act = project(up_ref)
            hidden = gate_act / (1.0 + jnp.exp(-gate_act)) * up_act
            hidden = jnp.where(weight > 0.0, hidden * weight, 0.0)
            columns = slice(e * units + at, e * units + at + block)
            row = 0
            for out_ref in out_refs:
                rows = slice(row, row + out_ref.shape[0])
                out_ref[:, columns] = hidden[rows].astype(jnp.bfloat16)
                row += out_ref.shape[0]


def hidden_kernel(half, experts, blocks, place_ref, *refs):
    gate_ref, up_ref, *out_refs = refs[2 * blocks : 2 * blocks + 4]
    own, other, coded = refs[2 * blocks + 4 :]
    fill_rows(half, blocks, refs, own, other, coded)
    hidden_units(half, experts, place_ref, gate_ref, up_ref, own, other, coded, out_refs)


def run_hidden(place, own, other, gate, up, experts, first):
    blocks = len(own)
    local, features, width = gate.shape
    rows, half, units = blocks * own[0].shape[0], features // 2, local * width
    vmem = pl.BlockSpec(memory_space=pltpu.VMEM)
    return pl.pallas_call(
        functools.partial(hidden_kernel, half, experts, blocks),
        out_shape=[
            jax.ShapeDtypeStruct((count * own[0].shape[0], units), jnp.bfloat16)
            for count in (first, blocks - first)
        ],
        in_specs=[pl.BlockSpec(memory_space=pltpu.SMEM)] + [vmem] * (2 * blocks + 2),
        out_specs=[vmem] * 2,
        scratch_shapes=[
            pltpu.VMEM((rows, half), jnp.bfloat16),
            pltpu.VMEM((rows, half), jnp.bfloat16),
            pltpu.VMEM((rows, own[0].shape[1] - half), jnp.float32),
        ],
        compiler_params=pltpu.CompilerParams(vmem_limit_bytes=LIMIT),
        cost_estimate=pl.CostEstimate(
            flops=4 * rows * units * features, bytes_accessed=4 * rows * half, transcendentals=rows * units
        ),
        name="hidden",
    )(place, *own, *other, gate, up)


def down_kernel(mine, place_ref, hidden_ref, down_ref, *refs):
    out_refs = refs[mine:]
    local, units, features = down_ref.shape
    half = features // 2
    core = place_ref[1] if mine else 1 - place_ref[1]
    tokens = out_refs[0].shape[0]
    for at in range(0, half, WIDTH):
        cut = pl.ds(pl.multiple_of(core * half + at, WIDTH), WIDTH)
        total = jnp.dot(
            hidden_ref[...],
            down_ref[:, :, cut].reshape(local * units, WIDTH),
            preferred_element_type=jnp.float32,
        )
        if mine:
            total = total + refs[0][:, at : at + WIDTH].astype(jnp.float32)
        for i, out_ref in enumerate(out_refs):
            out_ref[:, at : at + WIDTH] = total[i * tokens : (i + 1) * tokens].astype(out_ref.dtype)


def run_down(place, hidden, down, received, kinds):
    rows, half = hidden.shape[0], down.shape[2] // 2
    vmem = pl.BlockSpec(memory_space=pltpu.VMEM)
    extra = [] if received is None else [received]
    return pl.pallas_call(
        functools.partial(down_kernel, len(extra)),
        out_shape=[jax.ShapeDtypeStruct((rows // len(kinds), half), kind) for kind in kinds],
        in_specs=[pl.BlockSpec(memory_space=pltpu.SMEM)] + [vmem] * (2 + len(extra)),
        out_specs=[vmem] * len(kinds),
        compiler_params=pltpu.CompilerParams(vmem_limit_bytes=LIMIT),
        cost_estimate=pl.CostEstimate(
            flops=2 * rows * half, bytes_accessed=4 * rows, transcendentals=0
        ),
        name="mine" if extra else "other",
    )(place, hidden, down, *extra)


def after(value, *others):
    return lax.optimization_barrier((value, *others))[0]


def on_device(
    hidden_in, expert_ids, route_scores, expert_slot, gate_matrix, up_matrix, down_matrix
):
    token_count, feature_count = hidden_in.shape
    experts = expert_slot.shape[0]
    devices = lax.axis_size("sect")
    half = feature_count // 2
    core = lax.axis_index("tp")
    sect = lax.axis_index("sect")
    inner = 2
    outer = devices // inner

    def along(shift):
        return [
            (o * inner + i, (o + shift) % outer * inner + i)
            for o in range(outer)
            for i in range(inner)
        ]

    across = [(d, d ^ 1) for d in range(devices)]
    cores = [(0, 1), (1, 0)]
    place = jnp.stack([sect, core]).astype(jnp.int32)
    bf16, f32 = jnp.bfloat16, jnp.float32

    packed = prepare(place, hidden_in, expert_ids, route_scores, expert_slot)
    order = sorted(range(1, outer), key=lambda k: -min(k, outer - k))
    same, opposite = {0: packed}, {0: lax.ppermute(packed, "sect", across)}
    for k in order[::-1]:
        block = after(packed, opposite[0]) if k == order[0] and outer > 2 else packed
        same[k] = lax.ppermute(block, "sect", along(k))
    for k in order[::-1]:
        opposite[k] = lax.ppermute(same[k], "sect", across)
    blocks = [side[k] for side in (opposite, same) for k in range(outer)]
    others = [lax.ppermute(block, "tp", cores) for block in blocks]
    groups = run_hidden(place, blocks, others, gate_matrix, up_matrix, experts, outer)
    sent = [
        lax.ppermute(run_down(place, hidden, down_matrix, None, [bf16])[0], "tp", cores)
        for hidden in groups
    ]
    far_sum = run_down(place, groups[0], down_matrix, sent[0], [bf16] * outer)
    near_sum = run_down(place, groups[1], down_matrix, sent[1], [f32] * outer)
    result = lax.dynamic_slice_in_dim(hidden_in, core * half, half, 1).astype(f32)
    for k in order + [0]:
        block = near_sum[k] + lax.ppermute(far_sum[k], "sect", across).astype(f32)
        if k:
            block = lax.ppermute(block.astype(bf16), "sect", along(-k)).astype(f32)
        result = result + block
    return result.astype(bf16)


def solution(mesh):
    placed = (
        P(("groups", "sect"), None),
        P(("groups", "sect"), None),
        P(("groups", "sect"), None),
        P(),
        P("sect", None, "tp"),
        P("sect", None, "tp"),
        P("sect", "tp", None),
    )
    return jax.shard_map(
        on_device,
        mesh=mesh,
        in_specs=placed,
        out_specs=P(("groups", "sect"), "tp"),
        check_vma=False,
    )
```

```python
import functools

import jax
import jax.numpy as jnp
from jax import lax
from jax.experimental import pallas as pl
from jax.experimental.pallas import tpu as pltpu
from jax.sharding import PartitionSpec as P

LANES = 128
WIDTH = 512
LIMIT = 6 << 20
LEAD_FLOPS = 40_000_000_000


def prepare_kernel(half, experts, *refs):
    out_ref, slot_ref, hidden_ref, ids_ref, scores_ref, sem = refs[4:]
    copies = [
        pltpu.make_async_copy(refs[i], refs[5 + i], sem.at[i]) for i in range(4)
    ]
    for copy in copies:
        copy.start()
    for copy in copies:
        copy.wait()
    resid = hidden_ref[...].astype(jnp.float32)
    scale = lax.rsqrt(jnp.mean(resid * resid, axis=-1, keepdims=True) + 1e-06)
    own = hidden_ref[:, pl.ds(pl.multiple_of(lax.axis_index("tp") * half, half), half)]
    out_ref[:, :half] = (own.astype(jnp.float32) * scale).astype(jnp.bfloat16)
    scores = scores_ref[...]
    mixing = scores / jnp.sum(scores, axis=0, keepdims=True)
    ids = ids_ref[...]
    width = out_ref.shape[1] - half
    row = lax.broadcasted_iota(jnp.int32, (width, 1), 0)
    slot_of_row = lax.rem(row, experts)
    expert_of_row = jnp.zeros((width, 1), jnp.int32)
    for e in range(experts):
        expert_of_row = jnp.where(slot_of_row == slot_ref[e], e, expert_of_row)
    weight = jnp.zeros((width, ids.shape[1]), jnp.float32)
    for k in range(ids.shape[0]):
        weight = weight + jnp.where(ids[k : k + 1, :] == expert_of_row, mixing[k : k + 1, :], 0.0)
    high = weight.astype(jnp.bfloat16).astype(jnp.float32)
    middle = (weight - high).astype(jnp.bfloat16).astype(jnp.float32)
    low = weight - high - middle
    coded = jnp.where(
        row < experts,
        high,
        jnp.where(row < 2 * experts, middle, jnp.where(row < 3 * experts, low, 0.0)),
    )
    out_ref[:, half:] = coded.T.astype(jnp.bfloat16)


def prepare(hidden_in, expert_ids, route_scores, expert_slot):
    rows, features = hidden_in.shape
    half = features // 2
    experts = expert_slot.shape[0]
    width = -(-3 * experts // LANES) * LANES
    vmem = pl.BlockSpec(memory_space=pltpu.VMEM)
    hbm = pl.BlockSpec(memory_space=pltpu.HBM)
    far = [expert_slot, hidden_in, expert_ids.T, route_scores.T]
    far = [pltpu.with_memory_space_constraint(a, pltpu.HBM) for a in far]
    return pl.pallas_call(
        functools.partial(prepare_kernel, half, experts),
        out_shape=jax.ShapeDtypeStruct((rows, half + width), jnp.bfloat16),
        in_specs=[hbm] * 4,
        out_specs=vmem,
        scratch_shapes=[
            pltpu.SMEM(expert_slot.shape, jnp.int32),
            pltpu.VMEM(hidden_in.shape, hidden_in.dtype),
            pltpu.VMEM(expert_ids.shape[::-1], jnp.int32),
            pltpu.VMEM(route_scores.shape[::-1], jnp.float32),
            pltpu.SemaphoreType.DMA((4,)),
        ],
        compiler_params=pltpu.CompilerParams(vmem_limit_bytes=LIMIT),
        cost_estimate=pl.CostEstimate(
            flops=LEAD_FLOPS, bytes_accessed=2 * rows * features, transcendentals=0
        ),
        name="prepare",
    )(*far)


def fill_rows(half, blocks, refs, own, other, coded):
    tokens = refs[0].shape[0]
    for i in range(blocks):
        rows = slice(i * tokens, (i + 1) * tokens)
        own[rows, :] = refs[i][:, :half]
        other[rows, :] = refs[blocks + i][:, :half]
        coded[rows, :] = refs[i][:, half:].astype(jnp.float32)


def hidden_units(half, experts, gate_ref, up_ref, own, other, coded, out_refs):
    local, _, units = gate_ref.shape
    first_slot = lax.axis_index("sect") * local
    own_at = pl.ds(pl.multiple_of(lax.axis_index("tp") * half, half), half)
    other_at = pl.ds(pl.multiple_of((1 - lax.axis_index("tp")) * half, half), half)
    slot = lax.rem(lax.broadcasted_iota(jnp.int32, coded.shape, 1), experts)
    block = min(units, 256)
    for e in range(local):
        weight = jnp.sum(jnp.where(slot == first_slot + e, coded[...], 0.0), axis=1, keepdims=True)
        for at in range(0, units, block):
            cut = slice(at, at + block)

            def project(ref):
                return jnp.dot(
                    own[...], ref[e, own_at, cut], preferred_element_type=jnp.float32
                ) + jnp.dot(other[...], ref[e, other_at, cut], preferred_element_type=jnp.float32)

            gate_act = project(gate_ref)
            up_act = project(up_ref)
            hidden = gate_act / (1.0 + jnp.exp(-gate_act)) * up_act
            hidden = jnp.where(weight > 0.0, hidden * weight, 0.0)
            columns = slice(e * units + at, e * units + at + block)
            row = 0
            for out_ref in out_refs:
                rows = slice(row, row + out_ref.shape[0])
                out_ref[:, columns] = hidden[rows].astype(jnp.bfloat16)
                row += out_ref.shape[0]


def hidden_kernel(half, experts, blocks, *refs):
    gate_ref, up_ref, *out_refs = refs[2 * blocks : 2 * blocks + 4]
    own, other, coded = refs[2 * blocks + 4 :]
    fill_rows(half, blocks, refs, own, other, coded)
    hidden_units(half, experts, gate_ref, up_ref, own, other, coded, out_refs)


def run_hidden(own, other, gate, up, experts, first):
    blocks = len(own)
    local, features, width = gate.shape
    rows, half, units = blocks * own[0].shape[0], features // 2, local * width
    vmem = pl.BlockSpec(memory_space=pltpu.VMEM)
    return pl.pallas_call(
        functools.partial(hidden_kernel, half, experts, blocks),
        out_shape=[
            jax.ShapeDtypeStruct((count * own[0].shape[0], units), jnp.bfloat16)
            for count in (first, blocks - first)
        ],
        in_specs=[vmem] * (2 * blocks + 2),
        out_specs=[vmem] * 2,
        scratch_shapes=[
            pltpu.VMEM((rows, half), jnp.bfloat16),
            pltpu.VMEM((rows, half), jnp.bfloat16),
            pltpu.VMEM((rows, own[0].shape[1] - half), jnp.float32),
        ],
        compiler_params=pltpu.CompilerParams(vmem_limit_bytes=LIMIT),
        cost_estimate=pl.CostEstimate(
            flops=4 * rows * units * features, bytes_accessed=4 * rows * half, transcendentals=rows * units
        ),
        name="hidden",
    )(*own, *other, gate, up)


def down_kernel(mine, hidden_ref, down_ref, *refs):
    out_refs = refs[mine:]
    local, units, features = down_ref.shape
    half = features // 2
    core = lax.axis_index("tp") if mine else 1 - lax.axis_index("tp")
    tokens = out_refs[0].shape[0]
    for at in range(0, half, WIDTH):
        cut = pl.ds(pl.multiple_of(core * half + at, WIDTH), WIDTH)
        total = jnp.dot(
            hidden_ref[...],
            down_ref[:, :, cut].reshape(local * units, WIDTH),
            preferred_element_type=jnp.float32,
        )
        if mine:
            total = total + refs[0][:, at : at + WIDTH].astype(jnp.float32)
        for i, out_ref in enumerate(out_refs):
            out_ref[:, at : at + WIDTH] = total[i * tokens : (i + 1) * tokens].astype(out_ref.dtype)


def run_down(hidden, down, received, kinds):
    rows, half = hidden.shape[0], down.shape[2] // 2
    vmem = pl.BlockSpec(memory_space=pltpu.VMEM)
    extra = [] if received is None else [received]
    return pl.pallas_call(
        functools.partial(down_kernel, len(extra)),
        out_shape=[jax.ShapeDtypeStruct((rows // len(kinds), half), kind) for kind in kinds],
        in_specs=[vmem] * (2 + len(extra)),
        out_specs=[vmem] * len(kinds),
        compiler_params=pltpu.CompilerParams(vmem_limit_bytes=LIMIT),
        cost_estimate=pl.CostEstimate(
            flops=2 * rows * half, bytes_accessed=4 * rows, transcendentals=0
        ),
        name="mine" if extra else "other",
    )(hidden, down, *extra)


def after(value, *others):
    return lax.optimization_barrier((value, *others))[0]


def on_device(
    hidden_in, expert_ids, route_scores, expert_slot, gate_matrix, up_matrix, down_matrix
):
    token_count, feature_count = hidden_in.shape
    experts = expert_slot.shape[0]
    devices = lax.axis_size("sect")
    half = feature_count // 2
    core = lax.axis_index("tp")
    inner = 2
    outer = devices // inner

    def along(shift):
        return [
            (o * inner + i, (o + shift) % outer * inner + i)
            for o in range(outer)
            for i in range(inner)
        ]

    across = [(d, d ^ 1) for d in range(devices)]
    cores = [(0, 1), (1, 0)]
    bf16, f32 = jnp.bfloat16, jnp.float32

    packed = prepare(hidden_in, expert_ids, route_scores, expert_slot)
    order = sorted(range(1, outer), key=lambda k: -min(k, outer - k))
    same, opposite = {0: packed}, {0: lax.ppermute(packed, "sect", across)}
    for k in order[::-1]:
        block = after(packed, opposite[0]) if k == order[0] and outer > 2 else packed
        same[k] = lax.ppermute(block, "sect", along(k))
    for k in order[::-1]:
        opposite[k] = lax.ppermute(same[k], "sect", across)
    blocks = [side[k] for side in (opposite, same) for k in range(outer)]
    others = [lax.ppermute(block, "tp", cores) for block in blocks]
    groups = run_hidden(blocks, others, gate_matrix, up_matrix, experts, outer)
    sent = [
        lax.ppermute(run_down(hidden, down_matrix, None, [bf16])[0], "tp", cores)
        for hidden in groups
    ]
    far_sum = run_down(groups[0], down_matrix, sent[0], [bf16] * outer)
    near_sum = run_down(groups[1], down_matrix, sent[1], [f32] * outer)
    result = lax.dynamic_slice_in_dim(hidden_in, core * half, half, 1).astype(f32)
    for k in order + [0]:
        block = near_sum[k] + lax.ppermute(far_sum[k], "sect", across).astype(f32)
        if k:
            block = lax.ppermute(block.astype(bf16), "sect", along(-k)).astype(f32)
        result = result + block
    return result.astype(bf16)


def solution(mesh):
    placed = (
        P(("groups", "sect"), None),
        P(("groups", "sect"), None),
        P(("groups", "sect"), None),
        P(),
        P("sect", None, "tp"),
        P("sect", None, "tp"),
        P("sect", "tp", None),
    )
    return jax.shard_map(
        on_device,
        mesh=mesh,
        in_specs=placed,
        out_specs=P(("groups", "sect"), "tp"),
        check_vma=False,
    )
```

```python
import functools

import jax
import jax.numpy as jnp
from jax import lax
from jax.experimental import pallas as pl
from jax.experimental.pallas import tpu as pltpu
from jax.sharding import PartitionSpec as P

LANES = 128
WIDTH = 512
LIMIT = 6 << 20
LEAD_FLOPS = 40_000_000_000


def prepare_kernel(half, experts, *refs):
    out_ref, left_ref, right_ref, slot_ref, hidden_ref, ids_ref, scores_ref, sem = refs[4:]
    copies = [
        pltpu.make_async_copy(refs[i], refs[7 + i], sem.at[i]) for i in range(4)
    ]
    for copy in copies:
        copy.start()
    for copy in copies:
        copy.wait()
    resid = hidden_ref[...].astype(jnp.float32)
    scale = lax.rsqrt(jnp.mean(resid * resid, axis=-1, keepdims=True) + 1e-06)
    own = hidden_ref[:, pl.ds(pl.multiple_of(lax.axis_index("tp") * half, half), half)]
    out_ref[:, :half] = (own.astype(jnp.float32) * scale).astype(jnp.bfloat16)
    scores = scores_ref[...]
    mixing = scores / jnp.sum(scores, axis=0, keepdims=True)
    ids = ids_ref[...]
    width = out_ref.shape[1] - half
    row = lax.broadcasted_iota(jnp.int32, (width, 1), 0)
    slot_of_row = lax.rem(row, experts)
    expert_of_row = jnp.zeros((width, 1), jnp.int32)
    for e in range(experts):
        expert_of_row = jnp.where(slot_of_row == slot_ref[e], e, expert_of_row)
    weight = jnp.zeros((width, ids.shape[1]), jnp.float32)
    for k in range(ids.shape[0]):
        weight = weight + jnp.where(ids[k : k + 1, :] == expert_of_row, mixing[k : k + 1, :], 0.0)
    high = weight.astype(jnp.bfloat16).astype(jnp.float32)
    middle = (weight - high).astype(jnp.bfloat16).astype(jnp.float32)
    low = weight - high - middle
    coded = jnp.where(
        row < experts,
        high,
        jnp.where(row < 2 * experts, middle, jnp.where(row < 3 * experts, low, 0.0)),
    )
    out_ref[:, half:] = coded.T.astype(jnp.bfloat16)
    left = left_ref.shape[1]
    left_ref[...] = out_ref[:, :left]
    right_ref[...] = out_ref[:, left:]


def prepare(hidden_in, expert_ids, route_scores, expert_slot):
    rows, features = hidden_in.shape
    half = features // 2
    experts = expert_slot.shape[0]
    width = -(-3 * experts // LANES) * LANES
    vmem = pl.BlockSpec(memory_space=pltpu.VMEM)
    hbm = pl.BlockSpec(memory_space=pltpu.HBM)
    far = [expert_slot, hidden_in, expert_ids.T, route_scores.T]
    far = [pltpu.with_memory_space_constraint(a, pltpu.HBM) for a in far]
    return pl.pallas_call(
        functools.partial(prepare_kernel, half, experts),
        out_shape=[
            jax.ShapeDtypeStruct((rows, columns), jnp.bfloat16)
            for columns in (half + width, half // 2, half // 2 + width)
        ],
        in_specs=[hbm] * 4,
        out_specs=[vmem] * 3,
        scratch_shapes=[
            pltpu.SMEM(expert_slot.shape, jnp.int32),
            pltpu.VMEM(hidden_in.shape, hidden_in.dtype),
            pltpu.VMEM(expert_ids.shape[::-1], jnp.int32),
            pltpu.VMEM(route_scores.shape[::-1], jnp.float32),
            pltpu.SemaphoreType.DMA((4,)),
        ],
        compiler_params=pltpu.CompilerParams(vmem_limit_bytes=LIMIT),
        cost_estimate=pl.CostEstimate(
            flops=LEAD_FLOPS, bytes_accessed=2 * rows * features, transcendentals=0
        ),
        name="prepare",
    )(*far)


def fill_rows(half, pieces, own_refs, other_refs, own, other, coded):
    tokens = own_refs[0].shape[0]
    at = 0
    for i, count in enumerate(pieces):
        rows = slice(i * tokens, (i + 1) * tokens)
        column = 0
        for j in range(at, at + count):
            width = min(own_refs[j].shape[1], half - column)
            columns = slice(column, column + width)
            own[rows, columns] = own_refs[j][:, :width]
            other[rows, columns] = other_refs[j][:, :width]
            column += width
        coded[rows, :] = own_refs[at + count - 1][:, width:].astype(jnp.float32)
        at += count


def hidden_units(half, experts, gate_ref, up_ref, own, other, coded, out_refs):
    local, _, units = gate_ref.shape
    first_slot = lax.axis_index("sect") * local
    own_at = pl.ds(pl.multiple_of(lax.axis_index("tp") * half, half), half)
    other_at = pl.ds(pl.multiple_of((1 - lax.axis_index("tp")) * half, half), half)
    slot = lax.rem(lax.broadcasted_iota(jnp.int32, coded.shape, 1), experts)
    block = min(units, 256)
    for e in range(local):
        weight = jnp.sum(jnp.where(slot == first_slot + e, coded[...], 0.0), axis=1, keepdims=True)
        for at in range(0, units, block):
            cut = slice(at, at + block)

            def project(ref):
                return jnp.dot(
                    own[...], ref[e, own_at, cut], preferred_element_type=jnp.float32
                ) + jnp.dot(other[...], ref[e, other_at, cut], preferred_element_type=jnp.float32)

            gate_act = project(gate_ref)
            up_act = project(up_ref)
            hidden = gate_act / (1.0 + jnp.exp(-gate_act)) * up_act
            hidden = jnp.where(weight > 0.0, hidden * weight, 0.0)
            columns = slice(e * units + at, e * units + at + block)
            row = 0
            for out_ref in out_refs:
                rows = slice(row, row + out_ref.shape[0])
                out_ref[:, columns] = hidden[rows].astype(jnp.bfloat16)
                row += out_ref.shape[0]


def hidden_kernel(half, experts, pieces, *refs):
    count = sum(pieces)
    gate_ref, up_ref, *out_refs = refs[2 * count : 2 * count + 4]
    own, other, coded = refs[2 * count + 4 :]
    fill_rows(half, pieces, refs[:count], refs[count : 2 * count], own, other, coded)
    hidden_units(half, experts, gate_ref, up_ref, own, other, coded, out_refs)


def run_hidden(own, other, gate, up, experts, first):
    pieces = [len(block) for block in own]
    own = [piece for block in own for piece in block]
    other = [piece for block in other for piece in block]
    blocks, tokens = len(pieces), own[0].shape[0]
    local, features, width = gate.shape
    rows, half, units = blocks * tokens, features // 2, local * width
    coded = -(-3 * experts // LANES) * LANES
    vmem = pl.BlockSpec(memory_space=pltpu.VMEM)
    return pl.pallas_call(
        functools.partial(hidden_kernel, half, experts, pieces),
        out_shape=[
            jax.ShapeDtypeStruct((count * tokens, units), jnp.bfloat16)
            for count in (first, blocks - first)
        ],
        in_specs=[vmem] * (2 * len(own) + 2),
        out_specs=[vmem] * 2,
        scratch_shapes=[
            pltpu.VMEM((rows, half), jnp.bfloat16),
            pltpu.VMEM((rows, half), jnp.bfloat16),
            pltpu.VMEM((rows, coded), jnp.float32),
        ],
        compiler_params=pltpu.CompilerParams(vmem_limit_bytes=LIMIT),
        cost_estimate=pl.CostEstimate(
            flops=4 * rows * units * features, bytes_accessed=4 * rows * half, transcendentals=rows * units
        ),
        name="hidden",
    )(*own, *other, gate, up)


def down_kernel(mine, hidden_ref, down_ref, *refs):
    out_refs = refs[mine:]
    local, units, features = down_ref.shape
    half = features // 2
    core = lax.axis_index("tp") if mine else 1 - lax.axis_index("tp")
    tokens = out_refs[0].shape[0]
    for at in range(0, half, WIDTH):
        cut = pl.ds(pl.multiple_of(core * half + at, WIDTH), WIDTH)
        total = jnp.dot(
            hidden_ref[...],
            down_ref[:, :, cut].reshape(local * units, WIDTH),
            preferred_element_type=jnp.float32,
        )
        if mine:
            total = total + refs[0][:, at : at + WIDTH].astype(jnp.float32)
        for i, out_ref in enumerate(out_refs):
            out_ref[:, at : at + WIDTH] = total[i * tokens : (i + 1) * tokens].astype(out_ref.dtype)


def run_down(hidden, down, received, kinds):
    rows, half = hidden.shape[0], down.shape[2] // 2
    vmem = pl.BlockSpec(memory_space=pltpu.VMEM)
    extra = [] if received is None else [received]
    return pl.pallas_call(
        functools.partial(down_kernel, len(extra)),
        out_shape=[jax.ShapeDtypeStruct((rows // len(kinds), half), kind) for kind in kinds],
        in_specs=[vmem] * (2 + len(extra)),
        out_specs=[vmem] * len(kinds),
        compiler_params=pltpu.CompilerParams(vmem_limit_bytes=LIMIT),
        cost_estimate=pl.CostEstimate(
            flops=2 * rows * half, bytes_accessed=4 * rows, transcendentals=0
        ),
        name="mine" if extra else "other",
    )(hidden, down, *extra)


def after(value, *others):
    return lax.optimization_barrier((value, *others))[0]


def on_device(
    hidden_in, expert_ids, route_scores, expert_slot, gate_matrix, up_matrix, down_matrix
):
    token_count, feature_count = hidden_in.shape
    experts = expert_slot.shape[0]
    devices = lax.axis_size("sect")
    half = feature_count // 2
    core = lax.axis_index("tp")
    inner = 2
    outer = devices // inner

    def along(shift):
        return [
            (o * inner + i, (o + shift) % outer * inner + i)
            for o in range(outer)
            for i in range(inner)
        ]

    across = [(d, d ^ 1) for d in range(devices)]
    cores = [(0, 1), (1, 0)]
    bf16, f32 = jnp.bfloat16, jnp.float32

    packed, *halves = prepare(hidden_in, expert_ids, route_scores, expert_slot)
    order = sorted(range(1, outer), key=lambda k: -min(k, outer - k))
    crossed = lax.ppermute(packed, "sect", across)
    same, opposite = {0: [packed]}, {0: [crossed]}
    for k in order[::-1]:
        pieces = [packed]
        if k == order[0] and outer > 2:
            pieces = [after(piece, crossed) for piece in halves]
        same[k] = [lax.ppermute(piece, "sect", along(k)) for piece in pieces]
    for k in order[::-1]:
        opposite[k] = [lax.ppermute(piece, "sect", across) for piece in same[k]]
    blocks = [side[k] for side in (opposite, same) for k in range(outer)]
    others = [[lax.ppermute(piece, "tp", cores) for piece in block] for block in blocks]
    groups = run_hidden(blocks, others, gate_matrix, up_matrix, experts, outer)
    sent = [
        lax.ppermute(run_down(hidden, down_matrix, None, [bf16])[0], "tp", cores)
        for hidden in groups
    ]
    far_sum = run_down(groups[0], down_matrix, sent[0], [bf16] * outer)
    near_sum = run_down(groups[1], down_matrix, sent[1], [f32] * outer)
    result = lax.dynamic_slice_in_dim(hidden_in, core * half, half, 1).astype(f32)
    for k in order + [0]:
        block = near_sum[k] + lax.ppermute(far_sum[k], "sect", across).astype(f32)
        if k:
            block = lax.ppermute(block.astype(bf16), "sect", along(-k)).astype(f32)
        result = result + block
    return result.astype(bf16)


def solution(mesh):
    placed = (
        P(("groups", "sect"), None),
        P(("groups", "sect"), None),
        P(("groups", "sect"), None),
        P(),
        P("sect", None, "tp"),
        P("sect", None, "tp"),
        P("sect", "tp", None),
    )
    return jax.shard_map(
        on_device,
        mesh=mesh,
        in_specs=placed,
        out_specs=P(("groups", "sect"), "tp"),
        check_vma=False,
    )
```

```python
import functools

import jax
import jax.numpy as jnp
from jax import lax
from jax.experimental import pallas as pl
from jax.experimental.pallas import tpu as pltpu
from jax.sharding import PartitionSpec as P

LANES = 128
WIDTH = 512
LIMIT = 6 << 20
LEAD_FLOPS = 40_000_000_000


def prepare_kernel(half, experts, *refs):
    out_ref, slot_ref, hidden_ref, ids_ref, scores_ref, sem = refs[4:]
    copies = [
        pltpu.make_async_copy(refs[i], refs[5 + i], sem.at[i]) for i in range(4)
    ]
    for copy in copies:
        copy.start()
    for copy in copies:
        copy.wait()
    resid = hidden_ref[...].astype(jnp.float32)
    scale = lax.rsqrt(jnp.mean(resid * resid, axis=-1, keepdims=True) + 1e-06)
    own = hidden_ref[:, pl.ds(pl.multiple_of(lax.axis_index("tp") * half, half), half)]
    out_ref[:, :half] = (own.astype(jnp.float32) * scale).astype(jnp.bfloat16)
    scores = scores_ref[...]
    mixing = scores / jnp.sum(scores, axis=0, keepdims=True)
    ids = ids_ref[...]
    width = out_ref.shape[1] - half
    row = lax.broadcasted_iota(jnp.int32, (width, 1), 0)
    slot_of_row = lax.rem(row, experts)
    expert_of_row = jnp.zeros((width, 1), jnp.int32)
    for e in range(experts):
        expert_of_row = jnp.where(slot_of_row == slot_ref[e], e, expert_of_row)
    weight = jnp.zeros((width, ids.shape[1]), jnp.float32)
    for k in range(ids.shape[0]):
        weight = weight + jnp.where(ids[k : k + 1, :] == expert_of_row, mixing[k : k + 1, :], 0.0)
    high = weight.astype(jnp.bfloat16).astype(jnp.float32)
    middle = (weight - high).astype(jnp.bfloat16).astype(jnp.float32)
    low = weight - high - middle
    coded = jnp.where(
        row < experts,
        high,
        jnp.where(row < 2 * experts, middle, jnp.where(row < 3 * experts, low, 0.0)),
    )
    out_ref[:, half:] = coded.T.astype(jnp.bfloat16)


def prepare(hidden_in, expert_ids, route_scores, expert_slot):
    rows, features = hidden_in.shape
    half = features // 2
    experts = expert_slot.shape[0]
    width = -(-3 * experts // LANES) * LANES
    vmem = pl.BlockSpec(memory_space=pltpu.VMEM)
    hbm = pl.BlockSpec(memory_space=pltpu.HBM)
    far = [expert_slot, hidden_in, expert_ids.T, route_scores.T]
    far = [pltpu.with_memory_space_constraint(a, pltpu.HBM) for a in far]
    return pl.pallas_call(
        functools.partial(prepare_kernel, half, experts),
        out_shape=jax.ShapeDtypeStruct((rows, half + width), jnp.bfloat16),
        in_specs=[hbm] * 4,
        out_specs=vmem,
        scratch_shapes=[
            pltpu.SMEM(expert_slot.shape, jnp.int32),
            pltpu.VMEM(hidden_in.shape, hidden_in.dtype),
            pltpu.VMEM(expert_ids.shape[::-1], jnp.int32),
            pltpu.VMEM(route_scores.shape[::-1], jnp.float32),
            pltpu.SemaphoreType.DMA((4,)),
        ],
        compiler_params=pltpu.CompilerParams(vmem_limit_bytes=LIMIT),
        cost_estimate=pl.CostEstimate(
            flops=LEAD_FLOPS, bytes_accessed=2 * rows * features, transcendentals=0
        ),
        name="prepare",
    )(*far)


def fill_rows(half, blocks, refs, own, other, coded):
    tokens = refs[0].shape[0]
    for i in range(blocks):
        rows = slice(i * tokens, (i + 1) * tokens)
        own[rows, :] = refs[i][:, :half]
        other[rows, :] = refs[blocks + i][:, :half]
        coded[rows, :] = refs[i][:, half:].astype(jnp.float32)


def hidden_units(half, experts, gate_ref, up_ref, own, other, coded, out_refs):
    local, _, units = gate_ref.shape
    first_slot = lax.axis_index("sect") * local
    own_at = pl.ds(pl.multiple_of(lax.axis_index("tp") * half, half), half)
    other_at = pl.ds(pl.multiple_of((1 - lax.axis_index("tp")) * half, half), half)
    slot = lax.rem(lax.broadcasted_iota(jnp.int32, coded.shape, 1), experts)
    block = min(units, 256)
    for e in range(local):
        weight = jnp.sum(jnp.where(slot == first_slot + e, coded[...], 0.0), axis=1, keepdims=True)
        for at in range(0, units, block):
            cut = slice(at, at + block)

            def project(ref):
                return jnp.dot(
                    own[...], ref[e, own_at, cut], preferred_element_type=jnp.float32
                ) + jnp.dot(other[...], ref[e, other_at, cut], preferred_element_type=jnp.float32)

            gate_act = project(gate_ref)
            up_act = project(up_ref)
            hidden = gate_act / (1.0 + jnp.exp(-gate_act)) * up_act
            hidden = jnp.where(weight > 0.0, hidden * weight, 0.0)
            columns = slice(e * units + at, e * units + at + block)
            row = 0
            for out_ref in out_refs:
                rows = slice(row, row + out_ref.shape[0])
                out_ref[:, columns] = hidden[rows].astype(jnp.bfloat16)
                row += out_ref.shape[0]


def hidden_kernel(half, experts, blocks, *refs):
    gate_ref, up_ref, *out_refs = refs[2 * blocks : 2 * blocks + 4]
    own, other, coded = refs[2 * blocks + 4 :]
    fill_rows(half, blocks, refs, own, other, coded)
    hidden_units(half, experts, gate_ref, up_ref, own, other, coded, out_refs)


def run_hidden(own, other, gate, up, experts, first):
    blocks = len(own)
    local, features, width = gate.shape
    rows, half, units = blocks * own[0].shape[0], features // 2, local * width
    vmem = pl.BlockSpec(memory_space=pltpu.VMEM)
    return pl.pallas_call(
        functools.partial(hidden_kernel, half, experts, blocks),
        out_shape=[
            jax.ShapeDtypeStruct((count * own[0].shape[0], units), jnp.bfloat16)
            for count in (first, blocks - first)
        ],
        in_specs=[vmem] * (2 * blocks + 2),
        out_specs=[vmem] * 2,
        scratch_shapes=[
            pltpu.VMEM((rows, half), jnp.bfloat16),
            pltpu.VMEM((rows, half), jnp.bfloat16),
            pltpu.VMEM((rows, own[0].shape[1] - half), jnp.float32),
        ],
        compiler_params=pltpu.CompilerParams(vmem_limit_bytes=LIMIT),
        cost_estimate=pl.CostEstimate(
            flops=4 * rows * units * features, bytes_accessed=4 * rows * half, transcendentals=rows * units
        ),
        name="hidden",
    )(*own, *other, gate, up)


def down_kernel(mine, hidden_ref, down_ref, *refs):
    out_refs = refs[mine:]
    local, units, features = down_ref.shape
    half = features // 2
    core = lax.axis_index("tp") if mine else 1 - lax.axis_index("tp")
    tokens = out_refs[0].shape[0]
    for at in range(0, half, WIDTH):
        cut = pl.ds(pl.multiple_of(core * half + at, WIDTH), WIDTH)
        total = jnp.dot(
            hidden_ref[...],
            down_ref[:, :, cut].reshape(local * units, WIDTH),
            preferred_element_type=jnp.float32,
        )
        if mine:
            total = total + refs[0][:, at : at + WIDTH].astype(jnp.float32)
        for i, out_ref in enumerate(out_refs):
            out_ref[:, at : at + WIDTH] = total[i * tokens : (i + 1) * tokens].astype(out_ref.dtype)


def run_down(hidden, down, received, kinds):
    rows, half = hidden.shape[0], down.shape[2] // 2
    vmem = pl.BlockSpec(memory_space=pltpu.VMEM)
    extra = [] if received is None else [received]
    return pl.pallas_call(
        functools.partial(down_kernel, len(extra)),
        out_shape=[jax.ShapeDtypeStruct((rows // len(kinds), half), kind) for kind in kinds],
        in_specs=[vmem] * (2 + len(extra)),
        out_specs=[vmem] * len(kinds),
        compiler_params=pltpu.CompilerParams(vmem_limit_bytes=LIMIT),
        cost_estimate=pl.CostEstimate(
            flops=2 * rows * half, bytes_accessed=4 * rows, transcendentals=0
        ),
        name="mine" if extra else "other",
    )(hidden, down, *extra)


def after(value, *others):
    return lax.optimization_barrier((value, *others))[0]


def on_device(
    hidden_in, expert_ids, route_scores, expert_slot, gate_matrix, up_matrix, down_matrix
):
    token_count, feature_count = hidden_in.shape
    experts = expert_slot.shape[0]
    devices = lax.axis_size("sect")
    half = feature_count // 2
    core = lax.axis_index("tp")
    inner = 2
    outer = devices // inner

    def along(shift):
        return [
            (o * inner + i, (o + shift) % outer * inner + i)
            for o in range(outer)
            for i in range(inner)
        ]

    across = [(d, d ^ 1) for d in range(devices)]
    cores = [(0, 1), (1, 0)]
    bf16, f32 = jnp.bfloat16, jnp.float32

    packed = prepare(hidden_in, expert_ids, route_scores, expert_slot)
    order = sorted(range(1, outer), key=lambda k: -min(k, outer - k))
    same, opposite = {0: packed}, {}
    held = packed
    for k in order[::-1]:
        same[k] = lax.ppermute(held if k == order[0] else packed, "sect", along(k))
        if held is packed:
            held = after(packed, same[k])
    opposite[0] = lax.ppermute(held, "sect", across)
    for k in order[::-1]:
        opposite[k] = lax.ppermute(same[k], "sect", across)
    blocks = [side[k] for side in (opposite, same) for k in range(outer)]
    others = [lax.ppermute(block, "tp", cores) for block in blocks]
    groups = run_hidden(blocks, others, gate_matrix, up_matrix, experts, outer)
    sent = [
        lax.ppermute(run_down(hidden, down_matrix, None, [bf16])[0], "tp", cores)
        for hidden in groups
    ]
    far_sum = run_down(groups[0], down_matrix, sent[0], [bf16] * outer)
    near_sum = run_down(groups[1], down_matrix, sent[1], [f32] * outer)
    result = lax.dynamic_slice_in_dim(hidden_in, core * half, half, 1).astype(f32)
    for k in order + [0]:
        block = near_sum[k] + lax.ppermute(far_sum[k], "sect", across).astype(f32)
        if k:
            block = lax.ppermute(block.astype(bf16), "sect", along(-k)).astype(f32)
        result = result + block
    return result.astype(bf16)


def solution(mesh):
    placed = (
        P(("groups", "sect"), None),
        P(("groups", "sect"), None),
        P(("groups", "sect"), None),
        P(),
        P("sect", None, "tp"),
        P("sect", None, "tp"),
        P("sect", "tp", None),
    )
    return jax.shard_map(
        on_device,
        mesh=mesh,
        in_specs=placed,
        out_specs=P(("groups", "sect"), "tp"),
        check_vma=False,
    )
```

```python
import functools

import jax
import jax.numpy as jnp
from jax import lax
from jax.experimental import pallas as pl
from jax.experimental.pallas import tpu as pltpu
from jax.sharding import PartitionSpec as P

LANES = 128
WIDTH = 512
LIMIT = 6 << 20
LEAD_FLOPS = 40_000_000_000


def prepare_kernel(half, experts, *refs):
    out_ref, slot_ref, hidden_ref, ids_ref, scores_ref, sem = refs[4:]
    copies = [
        pltpu.make_async_copy(refs[i], refs[5 + i], sem.at[i]) for i in range(4)
    ]
    for copy in copies:
        copy.start()
    for copy in copies:
        copy.wait()
    resid = hidden_ref[...].astype(jnp.float32)
    scale = lax.rsqrt(jnp.mean(resid * resid, axis=-1, keepdims=True) + 1e-06)
    own = hidden_ref[:, pl.ds(pl.multiple_of(lax.axis_index("tp") * half, half), half)]
    out_ref[:, :half] = (own.astype(jnp.float32) * scale).astype(jnp.bfloat16)
    scores = scores_ref[...]
    mixing = scores / jnp.sum(scores, axis=0, keepdims=True)
    ids = ids_ref[...]
    width = out_ref.shape[1] - half
    row = lax.broadcasted_iota(jnp.int32, (width, 1), 0)
    slot_of_row = lax.rem(row, experts)
    expert_of_row = jnp.zeros((width, 1), jnp.int32)
    for e in range(experts):
        expert_of_row = jnp.where(slot_of_row == slot_ref[e], e, expert_of_row)
    weight = jnp.zeros((width, ids.shape[1]), jnp.float32)
    for k in range(ids.shape[0]):
        weight = weight + jnp.where(ids[k : k + 1, :] == expert_of_row, mixing[k : k + 1, :], 0.0)
    high = weight.astype(jnp.bfloat16).astype(jnp.float32)
    middle = (weight - high).astype(jnp.bfloat16).astype(jnp.float32)
    low = weight - high - middle
    coded = jnp.where(
        row < experts,
        high,
        jnp.where(row < 2 * experts, middle, jnp.where(row < 3 * experts, low, 0.0)),
    )
    out_ref[:, half:] = coded.T.astype(jnp.bfloat16)


def prepare(hidden_in, expert_ids, route_scores, expert_slot):
    rows, features = hidden_in.shape
    half = features // 2
    experts = expert_slot.shape[0]
    width = -(-3 * experts // LANES) * LANES
    vmem = pl.BlockSpec(memory_space=pltpu.VMEM)
    hbm = pl.BlockSpec(memory_space=pltpu.HBM)
    far = [expert_slot, hidden_in, expert_ids.T, route_scores.T]
    far = [pltpu.with_memory_space_constraint(a, pltpu.HBM) for a in far]
    return pl.pallas_call(
        functools.partial(prepare_kernel, half, experts),
        out_shape=jax.ShapeDtypeStruct((rows, half + width), jnp.bfloat16),
        in_specs=[hbm] * 4,
        out_specs=vmem,
        scratch_shapes=[
            pltpu.SMEM(expert_slot.shape, jnp.int32),
            pltpu.VMEM(hidden_in.shape, hidden_in.dtype),
            pltpu.VMEM(expert_ids.shape[::-1], jnp.int32),
            pltpu.VMEM(route_scores.shape[::-1], jnp.float32),
            pltpu.SemaphoreType.DMA((4,)),
        ],
        compiler_params=pltpu.CompilerParams(vmem_limit_bytes=LIMIT),
        cost_estimate=pl.CostEstimate(
            flops=LEAD_FLOPS, bytes_accessed=2 * rows * features, transcendentals=0
        ),
        name="prepare",
    )(*far)


def fill_rows(half, blocks, refs, own, other, coded):
    tokens = refs[0].shape[0]
    for i in range(blocks):
        rows = slice(i * tokens, (i + 1) * tokens)
        own[rows, :] = refs[i][:, :half]
        other[rows, :] = refs[blocks + i][:, :half]
        coded[rows, :] = refs[i][:, half:].astype(jnp.float32)


def hidden_units(half, experts, gate_ref, up_ref, own, other, coded, out_refs):
    local, _, units = gate_ref.shape
    first_slot = lax.axis_index("sect") * local
    own_at = pl.ds(pl.multiple_of(lax.axis_index("tp") * half, half), half)
    other_at = pl.ds(pl.multiple_of((1 - lax.axis_index("tp")) * half, half), half)
    slot = lax.rem(lax.broadcasted_iota(jnp.int32, coded.shape, 1), experts)
    block = min(units, 256)
    for e in range(local):
        weight = jnp.sum(jnp.where(slot == first_slot + e, coded[...], 0.0), axis=1, keepdims=True)
        for at in range(0, units, block):
            cut = slice(at, at + block)

            def project(ref):
                return jnp.dot(
                    own[...], ref[e, own_at, cut], preferred_element_type=jnp.float32
                ) + jnp.dot(other[...], ref[e, other_at, cut], preferred_element_type=jnp.float32)

            gate_act = project(gate_ref)
            up_act = project(up_ref)
            hidden = gate_act / (1.0 + jnp.exp(-gate_act)) * up_act
            hidden = jnp.where(weight > 0.0, hidden * weight, 0.0)
            columns = slice(e * units + at, e * units + at + block)
            row = 0
            for out_ref in out_refs:
                rows = slice(row, row + out_ref.shape[0])
                out_ref[:, columns] = hidden[rows].astype(jnp.bfloat16)
                row += out_ref.shape[0]


def hidden_kernel(half, experts, blocks, *refs):
    gate_ref, up_ref, *out_refs = refs[2 * blocks : 2 * blocks + 4]
    own, other, coded = refs[2 * blocks + 4 :]
    fill_rows(half, blocks, refs, own, other, coded)
    hidden_units(half, experts, gate_ref, up_ref, own, other, coded, out_refs)


def run_hidden(own, other, gate, up, experts, first):
    blocks = len(own)
    local, features, width = gate.shape
    rows, half, units = blocks * own[0].shape[0], features // 2, local * width
    vmem = pl.BlockSpec(memory_space=pltpu.VMEM)
    return pl.pallas_call(
        functools.partial(hidden_kernel, half, experts, blocks),
        out_shape=[
            jax.ShapeDtypeStruct((count * own[0].shape[0], units), jnp.bfloat16)
            for count in (first, blocks - first)
        ],
        in_specs=[vmem] * (2 * blocks + 2),
        out_specs=[vmem] * 2,
        scratch_shapes=[
            pltpu.VMEM((rows, half), jnp.bfloat16),
            pltpu.VMEM((rows, half), jnp.bfloat16),
            pltpu.VMEM((rows, own[0].shape[1] - half), jnp.float32),
        ],
        compiler_params=pltpu.CompilerParams(vmem_limit_bytes=LIMIT),
        cost_estimate=pl.CostEstimate(
            flops=4 * rows * units * features, bytes_accessed=4 * rows * half, transcendentals=rows * units
        ),
        name="hidden",
    )(*own, *other, gate, up)


def down_kernel(mine, hidden_ref, down_ref, *refs):
    out_refs = refs[mine:]
    local, units, features = down_ref.shape
    half = features // 2
    core = lax.axis_index("tp") if mine else 1 - lax.axis_index("tp")
    tokens = out_refs[0].shape[0]
    for at in range(0, half, WIDTH):
        cut = pl.ds(pl.multiple_of(core * half + at, WIDTH), WIDTH)
        total = jnp.dot(
            hidden_ref[...],
            down_ref[:, :, cut].reshape(local * units, WIDTH),
            preferred_element_type=jnp.float32,
        )
        if mine:
            total = total + refs[0][:, at : at + WIDTH].astype(jnp.float32)
        for i, out_ref in enumerate(out_refs):
            out_ref[:, at : at + WIDTH] = total[i * tokens : (i + 1) * tokens].astype(out_ref.dtype)


def run_down(hidden, down, received, kinds):
    rows, half = hidden.shape[0], down.shape[2] // 2
    vmem = pl.BlockSpec(memory_space=pltpu.VMEM)
    extra = [] if received is None else [received]
    return pl.pallas_call(
        functools.partial(down_kernel, len(extra)),
        out_shape=[jax.ShapeDtypeStruct((rows // len(kinds), half), kind) for kind in kinds],
        in_specs=[vmem] * (2 + len(extra)),
        out_specs=[vmem] * len(kinds),
        compiler_params=pltpu.CompilerParams(vmem_limit_bytes=LIMIT),
        cost_estimate=pl.CostEstimate(
            flops=2 * rows * half, bytes_accessed=4 * rows, transcendentals=0
        ),
        name="mine" if extra else "other",
    )(hidden, down, *extra)


def after(value, *others):
    return lax.optimization_barrier((value, *others))[0]


def on_device(
    hidden_in, expert_ids, route_scores, expert_slot, gate_matrix, up_matrix, down_matrix
):
    token_count, feature_count = hidden_in.shape
    experts = expert_slot.shape[0]
    devices = lax.axis_size("sect")
    half = feature_count // 2
    core = lax.axis_index("tp")
    inner = 2
    outer = devices // inner

    def along(shift):
        return [
            (o * inner + i, (o + shift) % outer * inner + i)
            for o in range(outer)
            for i in range(inner)
        ]

    across = [(d, d ^ 1) for d in range(devices)]
    cores = [(0, 1), (1, 0)]
    bf16, f32 = jnp.bfloat16, jnp.float32

    packed = prepare(hidden_in, expert_ids, route_scores, expert_slot)
    order = sorted(range(1, outer), key=lambda k: -min(k, outer - k))
    same, opposite = {0: packed}, {}
    held = packed
    for k in order[::-1]:
        same[k] = lax.ppermute(packed, "sect", along(k))
        if held is packed:
            held = after(packed, same[k])
    opposite[0] = lax.ppermute(held, "sect", across)
    for k in order[::-1]:
        opposite[k] = lax.ppermute(same[k], "sect", across)
    blocks = [side[k] for side in (opposite, same) for k in range(outer)]
    others = [lax.ppermute(block, "tp", cores) for block in blocks]
    groups = run_hidden(blocks, others, gate_matrix, up_matrix, experts, outer)
    sent = [
        lax.ppermute(run_down(hidden, down_matrix, None, [bf16])[0], "tp", cores)
        for hidden in groups
    ]
    far_sum = run_down(groups[0], down_matrix, sent[0], [bf16] * outer)
    near_sum = run_down(groups[1], down_matrix, sent[1], [f32] * outer)
    result = lax.dynamic_slice_in_dim(hidden_in, core * half, half, 1).astype(f32)
    for k in order + [0]:
        block = near_sum[k] + lax.ppermute(far_sum[k], "sect", across).astype(f32)
        if k:
            block = lax.ppermute(block.astype(bf16), "sect", along(-k)).astype(f32)
        result = result + block
    return result.astype(bf16)


def solution(mesh):
    placed = (
        P(("groups", "sect"), None),
        P(("groups", "sect"), None),
        P(("groups", "sect"), None),
        P(),
        P("sect", None, "tp"),
        P("sect", None, "tp"),
        P("sect", "tp", None),
    )
    return jax.shard_map(
        on_device,
        mesh=mesh,
        in_specs=placed,
        out_specs=P(("groups", "sect"), "tp"),
        check_vma=False,
    )
```

```python
import functools

import jax
import jax.numpy as jnp
from jax import lax
from jax.experimental import pallas as pl
from jax.experimental.pallas import tpu as pltpu
from jax.sharding import PartitionSpec as P

LANES = 128
WIDTH = 512
LIMIT = 6 << 20
LEAD_FLOPS = 40_000_000_000


def prepare_kernel(half, experts, *refs):
    out_ref, slot_ref, hidden_ref, ids_ref, scores_ref, sem = refs[4:]
    copies = [
        pltpu.make_async_copy(refs[i], refs[5 + i], sem.at[i]) for i in range(4)
    ]
    for copy in copies:
        copy.start()
    for copy in copies:
        copy.wait()
    resid = hidden_ref[...].astype(jnp.float32)
    scale = lax.rsqrt(jnp.mean(resid * resid, axis=-1, keepdims=True) + 1e-06)
    own = hidden_ref[:, pl.ds(pl.multiple_of(lax.axis_index("tp") * half, half), half)]
    out_ref[:, :half] = (own.astype(jnp.float32) * scale).astype(jnp.bfloat16)
    scores = scores_ref[...]
    mixing = scores / jnp.sum(scores, axis=0, keepdims=True)
    ids = ids_ref[...]
    width = out_ref.shape[1] - half
    row = lax.broadcasted_iota(jnp.int32, (width, 1), 0)
    slot_of_row = lax.rem(row, experts)
    expert_of_row = jnp.zeros((width, 1), jnp.int32)
    for e in range(experts):
        expert_of_row = jnp.where(slot_of_row == slot_ref[e], e, expert_of_row)
    weight = jnp.zeros((width, ids.shape[1]), jnp.float32)
    for k in range(ids.shape[0]):
        weight = weight + jnp.where(ids[k : k + 1, :] == expert_of_row, mixing[k : k + 1, :], 0.0)
    high = weight.astype(jnp.bfloat16).astype(jnp.float32)
    middle = (weight - high).astype(jnp.bfloat16).astype(jnp.float32)
    low = weight - high - middle
    coded = jnp.where(
        row < experts,
        high,
        jnp.where(row < 2 * experts, middle, jnp.where(row < 3 * experts, low, 0.0)),
    )
    out_ref[:, half:] = coded.T.astype(jnp.bfloat16)


def prepare(hidden_in, expert_ids, route_scores, expert_slot):
    rows, features = hidden_in.shape
    half = features // 2
    experts = expert_slot.shape[0]
    width = -(-3 * experts // LANES) * LANES
    vmem = pl.BlockSpec(memory_space=pltpu.VMEM)
    hbm = pl.BlockSpec(memory_space=pltpu.HBM)
    far = [expert_slot, hidden_in, expert_ids.T, route_scores.T]
    far = [pltpu.with_memory_space_constraint(a, pltpu.HBM) for a in far]
    return pl.pallas_call(
        functools.partial(prepare_kernel, half, experts),
        out_shape=jax.ShapeDtypeStruct((rows, half + width), jnp.bfloat16),
        in_specs=[hbm] * 4,
        out_specs=vmem,
        scratch_shapes=[
            pltpu.SMEM(expert_slot.shape, jnp.int32),
            pltpu.VMEM(hidden_in.shape, hidden_in.dtype),
            pltpu.VMEM(expert_ids.shape[::-1], jnp.int32),
            pltpu.VMEM(route_scores.shape[::-1], jnp.float32),
            pltpu.SemaphoreType.DMA((4,)),
        ],
        compiler_params=pltpu.CompilerParams(vmem_limit_bytes=LIMIT),
        cost_estimate=pl.CostEstimate(
            flops=LEAD_FLOPS, bytes_accessed=2 * rows * features, transcendentals=0
        ),
        name="prepare",
    )(*far)


def fill_rows(half, blocks, refs, own, other, coded):
    tokens = refs[0].shape[0]
    for i in range(blocks):
        rows = slice(i * tokens, (i + 1) * tokens)
        own[rows, :] = refs[i][:, :half]
        other[rows, :] = refs[blocks + i][:, :half]
        coded[rows, :] = refs[i][:, half:].astype(jnp.float32)


def hidden_units(half, experts, gate_ref, up_ref, own, other, coded, out_refs):
    local, _, units = gate_ref.shape
    first_slot = lax.axis_index("sect") * local
    own_at = pl.ds(pl.multiple_of(lax.axis_index("tp") * half, half), half)
    other_at = pl.ds(pl.multiple_of((1 - lax.axis_index("tp")) * half, half), half)
    slot = lax.rem(lax.broadcasted_iota(jnp.int32, coded.shape, 1), experts)
    block = min(units, 256)
    for e in range(local):
        weight = jnp.sum(jnp.where(slot == first_slot + e, coded[...], 0.0), axis=1, keepdims=True)
        for at in range(0, units, block):
            cut = slice(at, at + block)

            def project(ref):
                return jnp.dot(
                    own[...], ref[e, own_at, cut], preferred_element_type=jnp.float32
                ) + jnp.dot(other[...], ref[e, other_at, cut], preferred_element_type=jnp.float32)

            gate_act = project(gate_ref)
            up_act = project(up_ref)
            hidden = gate_act / (1.0 + jnp.exp(-gate_act)) * up_act
            hidden = jnp.where(weight > 0.0, hidden * weight, 0.0)
            columns = slice(e * units + at, e * units + at + block)
            row = 0
            for out_ref in out_refs:
                rows = slice(row, row + out_ref.shape[0])
                out_ref[:, columns] = hidden[rows].astype(jnp.bfloat16)
                row += out_ref.shape[0]


def hidden_kernel(half, experts, blocks, *refs):
    gate_ref, up_ref, *out_refs = refs[2 * blocks : 2 * blocks + 4]
    own, other, coded = refs[2 * blocks + 4 :]
    fill_rows(half, blocks, refs, own, other, coded)
    hidden_units(half, experts, gate_ref, up_ref, own, other, coded, out_refs)


def run_hidden(own, other, gate, up, experts, first):
    blocks = len(own)
    local, features, width = gate.shape
    rows, half, units = blocks * own[0].shape[0], features // 2, local * width
    vmem = pl.BlockSpec(memory_space=pltpu.VMEM)
    return pl.pallas_call(
        functools.partial(hidden_kernel, half, experts, blocks),
        out_shape=[
            jax.ShapeDtypeStruct((count * own[0].shape[0], units), jnp.bfloat16)
            for count in (first, blocks - first)
        ],
        in_specs=[vmem] * (2 * blocks + 2),
        out_specs=[vmem] * 2,
        scratch_shapes=[
            pltpu.VMEM((rows, half), jnp.bfloat16),
            pltpu.VMEM((rows, half), jnp.bfloat16),
            pltpu.VMEM((rows, own[0].shape[1] - half), jnp.float32),
        ],
        compiler_params=pltpu.CompilerParams(vmem_limit_bytes=LIMIT),
        cost_estimate=pl.CostEstimate(
            flops=4 * rows * units * features, bytes_accessed=4 * rows * half, transcendentals=rows * units
        ),
        name="hidden",
    )(*own, *other, gate, up)


def down_kernel(mine, hidden_ref, down_ref, *refs):
    out_refs = refs[mine:]
    local, units, features = down_ref.shape
    half = features // 2
    core = lax.axis_index("tp") if mine else 1 - lax.axis_index("tp")
    tokens = out_refs[0].shape[0]
    for at in range(0, half, WIDTH):
        cut = pl.ds(pl.multiple_of(core * half + at, WIDTH), WIDTH)
        total = jnp.dot(
            hidden_ref[...],
            down_ref[:, :, cut].reshape(local * units, WIDTH),
            preferred_element_type=jnp.float32,
        )
        if mine:
            total = total + refs[0][:, at : at + WIDTH].astype(jnp.float32)
        for i, out_ref in enumerate(out_refs):
            out_ref[:, at : at + WIDTH] = total[i * tokens : (i + 1) * tokens].astype(out_ref.dtype)


def run_down(hidden, down, received, kinds):
    rows, half = hidden.shape[0], down.shape[2] // 2
    vmem = pl.BlockSpec(memory_space=pltpu.VMEM)
    extra = [] if received is None else [received]
    return pl.pallas_call(
        functools.partial(down_kernel, len(extra)),
        out_shape=[jax.ShapeDtypeStruct((rows // len(kinds), half), kind) for kind in kinds],
        in_specs=[vmem] * (2 + len(extra)),
        out_specs=[vmem] * len(kinds),
        compiler_params=pltpu.CompilerParams(vmem_limit_bytes=LIMIT),
        cost_estimate=pl.CostEstimate(
            flops=2 * rows * half, bytes_accessed=4 * rows, transcendentals=0
        ),
        name="mine" if extra else "other",
    )(hidden, down, *extra)


def after(value, *others):
    return lax.optimization_barrier((value, *others))[0]


def on_device(
    hidden_in, expert_ids, route_scores, expert_slot, gate_matrix, up_matrix, down_matrix
):
    token_count, feature_count = hidden_in.shape
    experts = expert_slot.shape[0]
    devices = lax.axis_size("sect")
    half = feature_count // 2
    core = lax.axis_index("tp")
    inner = 2
    outer = devices // inner

    def along(shift):
        return [
            (o * inner + i, (o + shift) % outer * inner + i)
            for o in range(outer)
            for i in range(inner)
        ]

    across = [(d, d ^ 1) for d in range(devices)]
    cores = [(0, 1), (1, 0)]
    bf16, f32 = jnp.bfloat16, jnp.float32

    packed = prepare(hidden_in, expert_ids, route_scores, expert_slot)
    order = sorted(range(1, outer), key=lambda k: -min(k, outer - k))
    same, opposite = {0: packed}, {}
    for k in order[::-1]:
        same[k] = lax.ppermute(packed, "sect", along(k))
    own_other = lax.ppermute(packed, "tp", cores)
    opposite[0] = lax.ppermute(after(packed, own_other), "sect", across)
    for k in order[::-1]:
        opposite[k] = lax.ppermute(same[k], "sect", across)
    blocks = [side[k] for side in (opposite, same) for k in range(outer)]
    others = [
        own_other if block is packed else lax.ppermute(block, "tp", cores) for block in blocks
    ]
    groups = run_hidden(blocks, others, gate_matrix, up_matrix, experts, outer)
    sent = [
        lax.ppermute(run_down(hidden, down_matrix, None, [bf16])[0], "tp", cores)
        for hidden in groups
    ]
    far_sum = run_down(groups[0], down_matrix, sent[0], [bf16] * outer)
    near_sum = run_down(groups[1], down_matrix, sent[1], [f32] * outer)
    result = lax.dynamic_slice_in_dim(hidden_in, core * half, half, 1).astype(f32)
    for k in order + [0]:
        block = near_sum[k] + lax.ppermute(far_sum[k], "sect", across).astype(f32)
        if k:
            block = lax.ppermute(block.astype(bf16), "sect", along(-k)).astype(f32)
        result = result + block
    return result.astype(bf16)


def solution(mesh):
    placed = (
        P(("groups", "sect"), None),
        P(("groups", "sect"), None),
        P(("groups", "sect"), None),
        P(),
        P("sect", None, "tp"),
        P("sect", None, "tp"),
        P("sect", "tp", None),
    )
    return jax.shard_map(
        on_device,
        mesh=mesh,
        in_specs=placed,
        out_specs=P(("groups", "sect"), "tp"),
        check_vma=False,
    )
```
